128 devices in a mesh: rep: 4 (over z_lo, core), fsdp: 32 (over y, x, z_hi).
Axes of the slice: x: 4, y: 4, z: 4 (z_hi: 2, z_lo: 2; z = z_hi * 2 + z_lo), core: 2. Of those that a mesh axis runs over, the one named last changes fastest.
Arguments:
- activations: bfloat16 [4, 16384, 6144], P('rep', 'fsdp'), may hold values from -6 to 6
- cotangent: bfloat16 [4, 16384, 1024], P('rep', 'fsdp'), may hold values from -0.125 to 0.125
- weight: bfloat16 [4, 6144, 1024], P('rep', 'fsdp'), may hold values from -6 to 6
- first_moment: bfloat16 [4, 6144, 1024], P('rep', 'fsdp'), may hold values from -12 to 12
- second_moment: bfloat16 [4, 6144, 1024], P('rep', 'fsdp'), may hold values from 1 to 16
- anchor: bfloat16 [6144, 1024], P('fsdp'), may hold values from -6 to 6
- momentum: float32 [6144, 1024], P('fsdp'), may hold values from -6 to 6
- exponents: int32 [6144, 8], P('fsdp'), may hold values from -2 to 1
Outputs:
- new_weight: bfloat16 [4, 6144, 1024], P('rep', 'fsdp')
- new_first: bfloat16 [4, 6144, 1024], P('rep', 'fsdp')
- new_second: bfloat16 [4, 6144, 1024], P('rep', 'fsdp')
- new_anchor: bfloat16 [6144, 1024], P('fsdp')
- new_momentum: float32 [6144, 1024], P('fsdp')
The draws below stay inside these ranges and needn't reach their ends.
Inputs may be any that keep to these rules, and one draw needn't show every extreme that they name: `exponents`: one exponent for each block of 128 consecutive columns of a row.
All inputs are finite; a program needn't handle non-finite values.
Results may differ from the reference program's by a relative error of at most 0.02.
Values may be sent and summed in bfloat16 or wider, within the bound.
A program may use at most 128 MiB of HBM per device.

```python
import math
import jax
import jax.numpy as jnp

D = 6144
KV = 1024
TOKENS = 16384
REPS = 4
BLOCKS = 8
N_REP = 4


def touch_ends(array, key, least, top_value):
    index_at = [jax.random.randint(jax.random.fold_in(key, axis), (), 0, length) for axis, length in enumerate(array.shape)]
    longest = array.shape.index(max(array.shape))
    next_to = index_at[:longest] + [(index_at[longest] + 1) % array.shape[longest]] + index_at[longest + 1:]
    return array.at[tuple(index_at)].set(least).at[tuple(next_to)].set(top_value)


def with_spikes(drawn, own_key, source, target, shards_of, factor):
    owner, partner = [(jnp.arange(drawn.shape[dim]) // (drawn.shape[dim] // shards_of)).reshape([-1 if axis == dim else 1 for axis in range(drawn.ndim)]) for dim in (source, target)]
    chosen = jax.random.permutation(own_key, shards_of)[partner]
    strong = (owner == chosen) | (owner == (partner + shards_of // 2) % shards_of)
    return jnp.where(strong, factor * drawn, drawn)


def shard_levels(own_key, shape, cuts, least, largest):
    def one(dim, parts):
        heights = jax.random.uniform(jax.random.fold_in(jax.random.fold_in(own_key, 6), dim), (parts,), jnp.float32, least / len(cuts), largest / len(cuts))
        return jnp.repeat(jnp.exp(heights), shape[dim] // parts).reshape((-1,) + (1,) * (len(shape) - dim - 1))

    level = one(*cuts[0])
    for cut in cuts[1:]:
        level = level * one(*cut)
    return level


def bell_draw(own_key, extent, spread, reach, cuts=(), kind=jnp.bfloat16):
    values = spread * jax.random.normal(own_key, extent, jnp.float32)
    if cuts:
        values = values * shard_levels(own_key, extent, cuts, -0.22, 0.18)
    return jnp.clip(values, -reach, reach).astype(kind)


def noise_with(stream_key, dims, deviation, reach, cuts, heavy, kind=jnp.bfloat16):
    values = deviation * jax.random.normal(stream_key, dims, jnp.float32)
    if cuts:
        values = values * shard_levels(stream_key, dims, cuts, -0.22, 0.18)
    return jnp.clip(with_spikes(values, jax.random.fold_in(stream_key, 3), *heavy), -reach, reach).astype(kind)


def setup_inputs(seed: int = 0) -> dict:
    key_list = jax.random.split(jax.random.key(seed), 9)
    activations = noise_with(key_list[0], (REPS, TOKENS, D), 1.0, 6.0, ((0, 4), (1, 32)), (1, 2, 32, 2.75))
    cotangent = bell_draw(key_list[1], (REPS, TOKENS, KV), (TOKENS // 9) ** -0.5, 0.125, ((0, 4), (1, 32)))
    weight = bell_draw(key_list[2], (REPS, D, KV), 1.0, 6.0, ((0, 4), (1, 32)))
    first_moment = bell_draw(key_list[3], (REPS, D, KV), 2.0, 12.0, ((0, 4), (1, 32)))
    second_moment = jnp.clip(jnp.exp(math.log(16.0) - 2.7725887 * jax.random.uniform(key_list[4], (REPS, D, KV), jnp.float32) ** shard_levels(key_list[4], (REPS, D, KV), ((0, 4), (1, 32)), -0.2, 0.2)), 1.0, 16.0).astype(jnp.bfloat16)
    anchor = bell_draw(key_list[5], (D, KV), 1.0, 6.0, ((0, 32),))
    momentum = bell_draw(key_list[6], (D, KV), 1.0, 6.0, ((0, 32),), jnp.float32)
    exponents = touch_ends(jax.random.randint(key_list[7], (D, BLOCKS), -2, 2), jax.random.fold_in(key_list[7], 1), -2, 1).astype(jnp.int32)
    return dict(activations=activations, cotangent=cotangent, weight=weight, first_moment=first_moment, second_moment=second_moment, anchor=anchor, momentum=momentum, exponents=exponents)


def reference(activations, cotangent, weight, first_moment, second_moment, anchor, momentum, exponents):
    power = exponents.astype(jnp.float32)
    scale = jnp.repeat(jnp.exp2(power), 128, axis=1)
    inverse = jnp.repeat(jnp.exp2(-power), 128, axis=1)
    anchor_f = anchor.astype(jnp.float32)
    total = jnp.zeros(anchor.shape, jnp.float32)
    weights_out = []
    firsts_out = []
    seconds_out = []
    for replica in range(N_REP):
        grad = jnp.dot(activations[replica].T, cotangent[replica], preferred_element_type=jnp.float32)
        first = (0.9 * first_moment[replica].astype(jnp.float32) + 0.1 * grad).astype(jnp.bfloat16)
        second = (0.95 * second_moment[replica].astype(jnp.float32) + 0.05 * grad * grad).astype(jnp.bfloat16)
        old = weight[replica].astype(jnp.float32)
        update = first.astype(jnp.float32) / (jnp.sqrt(second.astype(jnp.float32)) + 1e-08)
        fresh = (old - 0.1 * (update + 0.01 * old)).astype(jnp.bfloat16)
        packed = jnp.clip((anchor_f - fresh.astype(jnp.float32)) * inverse, -4.0, 4.0).astype(jnp.bfloat16)
        total = total + packed.astype(jnp.float32)
        weights_out.append(fresh)
        firsts_out.append(first)
        seconds_out.append(second)
    outer = scale * total / N_REP
    new_momentum = 0.9 * momentum + outer
    new_anchor = (anchor_f - 0.7 * (outer + 0.9 * new_momentum)).astype(jnp.bfloat16)
    return (jnp.stack(weights_out), jnp.stack(firsts_out), jnp.stack(seconds_out), new_anchor, new_momentum)
```

```python
import jax
import jax.numpy as jnp
from jax import lax
from jax.experimental import pallas as pl
from jax.experimental.pallas import tpu as pltpu
from jax.sharding import PartitionSpec as P

MESH = pl.DeviceIdType.MESH
BF = jnp.bfloat16
F32 = jnp.float32

RING = 4
REPS = 4
GW = 256
OFFS = (2, 1, 3, 0)
A_SLOT = (0, 4, 2, 6)
B_SLOT = (3, 1, 5, 7)
NEW_BLOCKS = (
    ((0, 0), (0, 1), (0, 2), (1, 0), (2, 0)),
    ((1, 1), (1, 2), (2, 1)),
    ((2, 2), (0, 3), (3, 0)),
    ((3, 1), (3, 2), (1, 3), (2, 3), (3, 3)),
)


def plus(*terms):
    total = terms[0].astype(F32)
    for term in terms[1:]:
        total = total + term.astype(F32)
    return total


def kernel(act, cot, weight, first_in, second_in, anchor_in, mom_in, exps,
           w_out, f_out, s_out, anc_out, mom_out,
           a_v, c_v, w_v, f_v, s_v, anc_v, mom_v,
           part, rp, rm, fp, fm, part2, rp2, rm2, fp2, fm2, wsum, rz, packs,
           wo_v, fo_v, so_v, ao_v, mo_v,
           a_sem, c_sem, in_sem, out_sem,
           sp_s, sp_r, sm_s, sm_r, fp_s, fp_r, fm_s, fm_r,
           sp2_s, sp2_r, sm2_s, sm2_r, fp2_s, fp2_r, fm2_s, fm2_r,
           z_s, z_r, k_s, k_r):
    groups = c_v.shape[1] // GW
    own = w_v.shape[0]
    half = own // 2
    block = 2 * own
    rep = lax.axis_index("rep")
    f = lax.axis_index("fsdp")
    zlo, core = rep // 2, rep % 2
    zhi, x, y = f % 2, (f // 2) % RING, f // (2 * RING)

    def dev(x=x, y=y, zhi=zhi, rep=rep):
        return (rep, (y * RING + x) * 2 + zhi)

    xp, xm = dev(x=(x + 1) % RING), dev(x=(x + RING - 1) % RING)
    yp, ym = dev(y=(y + 1) % RING), dev(y=(y + RING - 1) % RING)
    zdev = dev(zhi=1 - zhi)
    mates = [dev(rep=(rep + i) % REPS) for i in range(1, REPS)]
    up1, down1 = (xp, yp), (xm, ym)
    up2, down2 = (yp, xp), (ym, xm)

    def cols(g):
        return pl.ds(pl.multiple_of(g * GW, GW), GW)

    def a_copy(blk):
        at = pl.ds(pl.multiple_of(blk * block, block), block)
        return pltpu.make_async_copy(act.at[0, :, at], a_v.at[:, at], a_sem.at[blk])

    def c_copy(g):
        return pltpu.make_async_copy(cot.at[0, :, cols(g)], c_v.at[:, cols(g)], c_sem.at[g])

    ins = [
        pltpu.make_async_copy(src, dst, in_sem.at[i])
        for i, (src, dst) in enumerate((
            (weight.at[0], w_v), (first_in.at[0], f_v), (second_in.at[0], s_v), (anchor_in, anc_v), (mom_in, mom_v)))
    ]

    def inner_outs(g):
        return [
            pltpu.make_async_copy(src.at[:, cols(g)], dst.at[0, :, cols(g)], out_sem.at[i, g])
            for i, (src, dst) in enumerate(((wo_v, w_out), (fo_v, f_out), (so_v, s_out)))
        ]

    def outer_outs(g):
        return [
            pltpu.make_async_copy(src.at[:, cols(g)], dst.at[:, cols(g)], out_sem.at[3 + i, g])
            for i, (src, dst) in enumerate(((ao_v, anc_out), (mo_v, mom_out)))
        ]

    def remote(src, dst, s, r, to):
        return pltpu.make_async_remote_copy(
            src_ref=src, dst_ref=dst, send_sem=s, recv_sem=r, device_id=to, device_id_type=MESH)

    def c_sp(h, g, k):
        return remote(part.at[h, g, k, pl.ds(0, 2)], rp.at[h, g, k], sp_s.at[h, g, k], sp_r.at[h, g, k], up1[h])

    def c_sm(h, g, k):
        return remote(part.at[h, g, k, pl.ds(2, 2)], rm.at[h, g, k], sm_s.at[h, g, k], sm_r.at[h, g, k], down1[h])

    def c_fp(h, g, k):
        return remote(rp.at[h, g, k, 0], fp.at[h, g, k], fp_s.at[h, g, k], fp_r.at[h, g, k], up1[h])

    def c_fm(h, g, k):
        return remote(rm.at[h, g, k, 1], fm.at[h, g, k], fm_s.at[h, g, k], fm_r.at[h, g, k], down1[h])

    def c_sp2(h, g):
        return remote(part2.at[h, g, pl.ds(0, 2)], rp2.at[h, g], sp2_s.at[h, g], sp2_r.at[h, g], up2[h])

    def c_sm2(h, g):
        return remote(part2.at[h, g, pl.ds(2, 2)], rm2.at[h, g], sm2_s.at[h, g], sm2_r.at[h, g], down2[h])

    def c_fp2(h, g):
        return remote(rp2.at[h, g, 0], fp2.at[h, g], fp2_s.at[h, g], fp2_r.at[h, g], up2[h])

    def c_fm2(h, g):
        return remote(rm2.at[h, g, 1], fm2.at[h, g], fm2_s.at[h, g], fm2_r.at[h, g], down2[h])

    def c_z(g):
        return remote(wsum.at[1 - zhi, g], rz.at[g], z_s.at[g], z_r.at[g], zdev)

    def c_pack(g, i):
        return remote(packs.at[g, rep], packs.at[g, rep], k_s.at[g, i], k_r.at[g, i], mates[i])

    def products(g, k):
        @pl.when(g == 0)
        def _():
            for ry, rx in NEW_BLOCKS[k]:
                a_copy(((y + OFFS[ry]) % RING) * RING + (x + OFFS[rx]) % RING).wait()

        if k == 0:
            c_copy(g).wait()
        right = c_v[:, cols(g)]
        for ry, rx in NEW_BLOCKS[k]:
            blk = ((y + OFFS[ry]) % RING) * RING + (x + OFFS[rx]) % RING
            at = pl.ds(pl.multiple_of(blk * block, block), block)
            tile = lax.dot_general(
                a_v[:, at], right, (((0,), (0,)), ((), ())), preferred_element_type=F32).astype(BF)
            part[0, g, ry, A_SLOT[rx]] = tile[:half]
            part[0, g, ry, B_SLOT[rx]] = tile[half:own]
            part[1, g, rx, A_SLOT[ry]] = tile[own:own + half]
            part[1, g, rx, B_SLOT[ry]] = tile[own + half:]
        for h in range(2):
            c_sp(h, g, k).start()
            c_sm(h, g, k).start()

    def forward(g, k):
        for h in range(2):
            c_sp(h, g, k).wait_recv()
            rp[h, g, k, 0] = plus(rp[h, g, k, 0], part[h, g, k, 4]).astype(BF)
            c_fp(h, g, k).start()
            c_sm(h, g, k).wait_recv()
            rm[h, g, k, 1] = plus(rm[h, g, k, 1], part[h, g, k, 5]).astype(BF)
            c_fm(h, g, k).start()

    def first_sum(g, k):
        for h in range(2):
            c_fp(h, g, k).wait_recv()
            c_fm(h, g, k).wait_recv()
            part2[h, g, A_SLOT[k]] = plus(part[h, g, k, 6], fp[h, g, k], rm[h, g, k, 0]).astype(BF)
            part2[h, g, B_SLOT[k]] = plus(part[h, g, k, 7], fm[h, g, k], rp[h, g, k, 1]).astype(BF)
            if k == 2:
                c_sp2(h, g).start()
                c_sm2(h, g).start()

    def forward2(g):
        for h in range(2):
            c_sp2(h, g).wait_recv()
            rp2[h, g, 0] = plus(rp2[h, g, 0], part2[h, g, 4]).astype(BF)
            c_fp2(h, g).start()
            c_sm2(h, g).wait_recv()
            rm2[h, g, 1] = plus(rm2[h, g, 1], part2[h, g, 5]).astype(BF)
            c_fm2(h, g).start()

    def second_sum(g):
        for h in range(2):
            c_fp2(h, g).wait_recv()
            c_fm2(h, g).wait_recv()
            wsum[h, g, pl.ds(0, half)] = plus(part2[h, g, 6], fp2[h, g], rm2[h, g, 0]).astype(BF)
            wsum[h, g, pl.ds(half, half)] = plus(part2[h, g, 7], fm2[h, g], rp2[h, g, 1]).astype(BF)
        c_z(g).start()

    def powers(g):
        lane = lax.broadcasted_iota(jnp.int32, exps.shape, 1)
        per = GW // 128
        parts = []
        for i in range(per):
            one = jnp.sum(jnp.where(lane == g * per + i, exps[...].astype(F32), 0.0), axis=1, keepdims=True)
            parts.append(jnp.broadcast_to(one, (own, 128)))
        return jnp.concatenate(parts, axis=1)

    def inner(g):
        c_z(g).wait_recv()
        @pl.when(g == 0)
        def _():
            for copy in ins:
                copy.wait()
        at = cols(g)
        grad = plus(wsum[zhi, g], rz[g])
        first = (0.9 * f_v[:, at].astype(F32) + 0.1 * grad).astype(BF)
        second = (0.95 * s_v[:, at].astype(F32) + 0.05 * grad * grad).astype(BF)
        old = w_v[:, at].astype(F32)
        update = first.astype(F32) / (jnp.sqrt(second.astype(F32)) + 1e-08)
        fresh = (old - 0.1 * (update + 0.01 * old)).astype(BF)
        fo_v[:, at] = first
        so_v[:, at] = second
        wo_v[:, at] = fresh
        gap = anc_v[:, at].astype(F32) - fresh.astype(F32)
        packs[g, rep] = jnp.clip(gap * jnp.exp2(-powers(g)), -4.0, 4.0).astype(BF)
        for i in range(REPS - 1):
            c_pack(g, i).start()
        for copy in inner_outs(g):
            copy.start()

    def outer(g):
        for i in range(REPS - 1):
            c_pack(g, i).wait_recv()
        at = cols(g)
        total = plus(*[packs[g, i] for i in range(REPS)])
        step = (jnp.exp2(powers(g)) * total) / REPS
        momentum = 0.9 * mom_v[:, at] + step
        mo_v[:, at] = momentum
        ao_v[:, at] = (anc_v[:, at].astype(F32) - 0.7 * (step + 0.9 * momentum)).astype(BF)
        for copy in outer_outs(g):
            copy.start()

    c_copy(0).start()
    for k in range(4):
        for ry, rx in NEW_BLOCKS[k]:
            a_copy(((y + OFFS[ry]) % RING) * RING + (x + OFFS[rx]) % RING).start()
    for g in range(1, groups):
        c_copy(g).start()
    for copy in ins:
        copy.start()

    everyone = [xp, xm, yp, ym, zdev] + mates
    barrier = pltpu.get_barrier_semaphore()
    for to in everyone:
        pl.semaphore_signal(barrier, inc=1, device_id=to, device_id_type=MESH)
    pl.semaphore_wait(barrier, len(everyone))

    @pl.loop(0, groups + 2)
    def _(turn):
        g = turn - 1
        for k in range(4):
            ahead, k2 = g + (k + 2) // 4, (k + 2) % 4
            nxt, k1 = g + (k + 1) // 4, (k + 1) % 4

            @pl.when(jnp.logical_and(ahead >= 0, ahead < groups))
            def _():
                products(ahead, k2)

            @pl.when(jnp.logical_and(nxt >= 0, nxt < groups))
            def _():
                forward(nxt, k1)

            @pl.when(jnp.logical_and(g >= 0, g < groups))
            def _():
                first_sum(g, k)
                if k == 3:
                    forward2(g)

            if k < 3:
                @pl.when(g >= 1)
                def _():
                    (second_sum, inner, outer)[k](g - 1)

    @pl.loop(0, groups)
    def _(g):
        for h in range(2):
            for k in range(4):
                c_sp(h, g, k).wait_send()
                c_sm(h, g, k).wait_send()
                c_fp(h, g, k).wait_send()
                c_fm(h, g, k).wait_send()
            c_sp2(h, g).wait_send()
            c_sm2(h, g).wait_send()
            c_fp2(h, g).wait_send()
            c_fm2(h, g).wait_send()
        c_z(g).wait_send()
        for i in range(REPS - 1):
            c_pack(g, i).wait_send()
        for copy in inner_outs(g) + outer_outs(g):
            copy.wait()


def local(activations, cotangent, weight, first_moment, second_moment, anchor, momentum, exponents):
    own, width = anchor.shape
    tokens, rows = activations.shape[1:]
    groups = width // GW
    half = own // 2
    dma = pltpu.SemaphoreType.DMA
    anywhere = pl.BlockSpec(memory_space=pl.ANY)

    def buf(*shape, kind=BF):
        return pltpu.VMEM(shape, kind)

    return pl.pallas_call(
        kernel,
        out_shape=(
            jax.ShapeDtypeStruct(weight.shape, BF),
            jax.ShapeDtypeStruct(weight.shape, BF),
            jax.ShapeDtypeStruct(weight.shape, BF),
            jax.ShapeDtypeStruct(anchor.shape, BF),
            jax.ShapeDtypeStruct(momentum.shape, F32),
        ),
        in_specs=[anywhere] * 7 + [pl.BlockSpec(memory_space=pltpu.VMEM)],
        out_specs=[anywhere] * 5,
        scratch_shapes=[
            buf(tokens, rows), buf(tokens, width),
            buf(own, width), buf(own, width), buf(own, width), buf(own, width), buf(own, width, kind=F32),
            buf(2, groups, 4, 8, half, GW),
            buf(2, groups, 4, 2, half, GW), buf(2, groups, 4, 2, half, GW),
            buf(2, groups, 4, half, GW), buf(2, groups, 4, half, GW),
            buf(2, groups, 8, half, GW),
            buf(2, groups, 2, half, GW), buf(2, groups, 2, half, GW),
            buf(2, groups, half, GW), buf(2, groups, half, GW),
            buf(2, groups, own, GW), buf(groups, own, GW), buf(groups, REPS, own, GW),
            buf(own, width), buf(own, width), buf(own, width), buf(own, width), buf(own, width, kind=F32),
            dma((RING * RING,)), dma((groups,)), dma((5,)), dma((5, groups)),
        ] + [dma((2, groups, 4))] * 8 + [dma((2, groups))] * 8
        + [dma((groups,))] * 2 + [dma((groups, REPS - 1))] * 2,
        compiler_params=pltpu.CompilerParams(
            collective_id=0, has_side_effects=True, vmem_limit_bytes=58 * 1024 * 1024),
        cost_estimate=pl.CostEstimate(
            flops=2 * tokens * rows * width, bytes_accessed=12 * 2 ** 20, transcendentals=0),
        name="diloco_step",
    )(activations, cotangent, weight, first_moment, second_moment, anchor, momentum, exponents)


def solution(mesh):
    split = P("rep", "fsdp", None)
    rows = P("fsdp", None)
    return jax.shard_map(
        local,
        mesh=mesh,
        in_specs=(split, split, split, split, split, rows, rows, rows),
        out_specs=(split, split, split, rows, rows),
        check_vma=False,
    )
```

```python
import jax
import jax.numpy as jnp
from jax import lax
from jax.experimental import pallas as pl
from jax.experimental.pallas import tpu as pltpu
from jax.sharding import PartitionSpec as P

MESH = pl.DeviceIdType.MESH
BF = jnp.bfloat16
F32 = jnp.float32

RING = 4
REPS = 4
GW = 256
LEAD = 4
FLEAD = 2
LAGS = (1,3,5,7)
OFFS = (2, 1, 3, 0)
A_SLOT = (0, 4, 2, 6)
B_SLOT = (3, 1, 5, 7)
NEW_BLOCKS = (
    ((0, 0), (0, 1), (0, 2), (1, 0), (2, 0)),
    ((1, 1), (1, 2), (2, 1)),
    ((2, 2), (0, 3), (3, 0)),
    ((3, 1), (3, 2), (1, 3), (2, 3), (3, 3)),
)


def plus(*terms):
    total = terms[0].astype(F32)
    for term in terms[1:]:
        total = total + term.astype(F32)
    return total


class Rings:
    def __init__(self, refs, up, down, remote):
        (self.part, self.rp, self.rm, self.fp, self.fm, self.part2, self.rp2, self.rm2, self.fp2, self.fm2) = refs[:10]
        self.sems = refs[10:]
        self.up, self.down, self.remote = up, down, remote
        self.unit = self.part.shape[-2]

    def copy(self, which, h, g, k):
        part, sems = self.part, self.sems
        if which < 4:
            at, up, down = (h, g, k), self.up[h], self.down[h]
            rp, rm, fp, fm = self.rp, self.rm, self.fp, self.fm
        else:
            part, at, up, down = self.part2, (h, g), self.up[1 - h], self.down[1 - h]
            rp, rm, fp, fm = self.rp2, self.rm2, self.fp2, self.fm2
        src, dst, to = (
            (part.at[(*at, pl.ds(0, 2))], rp.at[at], up),
            (part.at[(*at, pl.ds(2, 2))], rm.at[at], down),
            (rp.at[(*at, 0)], fp.at[at], up),
            (rm.at[(*at, 1)], fm.at[at], down),
        )[which % 4]
        return self.remote(src, dst, sems[2 * which].at[at], sems[2 * which + 1].at[at], to)

    def place(self, g, ry, rx, tile):
        u = self.unit
        self.part[0, g, ry, A_SLOT[rx]] = tile[:u]
        self.part[0, g, ry, B_SLOT[rx]] = tile[u:2 * u]
        self.part[1, g, rx, A_SLOT[ry]] = tile[2 * u:3 * u]
        self.part[1, g, rx, B_SLOT[ry]] = tile[3 * u:]

    def send(self, g, k):
        for h in range(2):
            self.copy(0, h, g, k).start()
            self.copy(1, h, g, k).start()

    def forward(self, g, k):
        for h in range(2):
            self.copy(0, h, g, k).wait_recv()
            self.rp[h, g, k, 0] = plus(self.rp[h, g, k, 0], self.part[h, g, k, 4]).astype(BF)
            self.copy(2, h, g, k).start()
            self.copy(1, h, g, k).wait_recv()
            self.rm[h, g, k, 1] = plus(self.rm[h, g, k, 1], self.part[h, g, k, 5]).astype(BF)
            self.copy(3, h, g, k).start()

    def first_sum(self, g, k):
        for h in range(2):
            self.copy(2, h, g, k).wait_recv()
            self.copy(3, h, g, k).wait_recv()
            self.part2[h, g, A_SLOT[k]] = plus(
                self.part[h, g, k, 6], self.fp[h, g, k], self.rm[h, g, k, 0]).astype(BF)
            self.part2[h, g, B_SLOT[k]] = plus(
                self.part[h, g, k, 7], self.fm[h, g, k], self.rp[h, g, k, 1]).astype(BF)
            if k == 2:
                self.copy(4, h, g, 0).start()
                self.copy(5, h, g, 0).start()

    def forward2(self, g):
        for h in range(2):
            self.copy(4, h, g, 0).wait_recv()
            self.rp2[h, g, 0] = plus(self.rp2[h, g, 0], self.part2[h, g, 4]).astype(BF)
            self.copy(6, h, g, 0).start()
            self.copy(5, h, g, 0).wait_recv()
            self.rm2[h, g, 1] = plus(self.rm2[h, g, 1], self.part2[h, g, 5]).astype(BF)
            self.copy(7, h, g, 0).start()

    def second_sum(self, h, g):
        self.copy(6, h, g, 0).wait_recv()
        self.copy(7, h, g, 0).wait_recv()
        return [
            plus(self.part2[h, g, 6], self.fp2[h, g], self.rm2[h, g, 0]),
            plus(self.part2[h, g, 7], self.fm2[h, g], self.rp2[h, g, 1]),
        ]

    def drain(self, g):
        for h in range(2):
            for k in range(RING):
                for which in range(4):
                    self.copy(which, h, g, k).wait_send()
            for which in range(4, 8):
                self.copy(which, h, g, 0).wait_send()


def kernel(act, cot, weight, first_in, second_in, anchor_in, mom_in, exps,
           w_out, f_out, s_out, anc_out, mom_out,
           a_v, c_v, w_v, f_v, s_v, anc_v, mom_v, wo_v, fo_v, so_v, ao_v, mo_v,
           wsum, rz, zt, zr, packs,
           a_sem, c_sem, in_sem, out_sem, z_s, z_r, zx_s, zx_r, k_s, k_r, *ring_refs):
    groups = c_v.shape[1] // GW
    last = groups - 1
    own = w_v.shape[0]
    block = 2 * own
    rep = lax.axis_index("rep")
    f = lax.axis_index("fsdp")
    zhi, x, y = f % 2, (f // 2) % RING, f // (2 * RING)

    def dev(x=x, y=y, zhi=zhi, rep=rep):
        return (rep, (y * RING + x) * 2 + zhi)

    xp, xm = dev(x=(x + 1) % RING), dev(x=(x + RING - 1) % RING)
    yp, ym = dev(y=(y + 1) % RING), dev(y=(y + RING - 1) % RING)
    zdev = dev(zhi=1 - zhi)
    mates = [dev(rep=(rep + i) % REPS) for i in range(1, REPS)]

    def cols(g):
        return pl.ds(pl.multiple_of(g * GW, GW), GW)

    def a_copy(blk):
        at = pl.ds(pl.multiple_of(blk * block, block), block)
        return pltpu.make_async_copy(act.at[0, :, at], a_v.at[:, at], a_sem.at[blk])

    def c_copy(g):
        return pltpu.make_async_copy(cot.at[0, :, cols(g)], c_v.at[:, cols(g)], c_sem.at[g])

    ins = [
        pltpu.make_async_copy(src, dst, in_sem.at[i])
        for i, (src, dst) in enumerate((
            (weight.at[0], w_v), (first_in.at[0], f_v), (second_in.at[0], s_v), (anchor_in, anc_v), (mom_in, mom_v)))
    ]

    def inner_outs(g):
        return [
            pltpu.make_async_copy(src.at[:, cols(g)], dst.at[0, :, cols(g)], out_sem.at[i, g])
            for i, (src, dst) in enumerate(((wo_v, w_out), (fo_v, f_out), (so_v, s_out)))
        ]

    def outer_outs(g):
        return [
            pltpu.make_async_copy(src.at[:, cols(g)], dst.at[:, cols(g)], out_sem.at[3 + i, g])
            for i, (src, dst) in enumerate(((ao_v, anc_out), (mo_v, mom_out)))
        ]

    def remote(src, dst, s, r, to):
        return pltpu.make_async_remote_copy(
            src_ref=src, dst_ref=dst, send_sem=s, recv_sem=r, device_id=to, device_id_type=MESH)

    def c_z(g):
        return remote(wsum.at[1 - zhi, g], rz.at[g], z_s.at[g], z_r.at[g], zdev)

    def c_zx(ry, rx):
        return remote(zt.at[ry, rx, 1 - zhi], zr.at[ry, rx], zx_s.at[ry, rx], zx_r.at[ry, rx], zdev)

    def c_pack(g, i):
        return remote(packs.at[g, rep], packs.at[g, rep], k_s.at[g, i], k_r.at[g, i], mates[i])

    wide = Rings(ring_refs[:26], (xp, yp), (xm, ym), remote)
    thin = Rings(ring_refs[26:], (xp, yp), (xm, ym), remote)

    def product(g, ry, rx):
        blk = ((y + OFFS[ry]) % RING) * RING + (x + OFFS[rx]) % RING
        at = pl.ds(pl.multiple_of(blk * block, block), block)
        return lax.dot_general(
            a_v[:, at], c_v[:, cols(g)], (((0,), (0,)), ((), ())), preferred_element_type=F32).astype(BF)

    def products(g, k):
        @pl.when(g == 0)
        def _():
            for ry, rx in NEW_BLOCKS[k]:
                a_copy(((y + OFFS[ry]) % RING) * RING + (x + OFFS[rx]) % RING).wait()

        if k == 0:
            c_copy(g).wait()
        for ry, rx in NEW_BLOCKS[k]:
            wide.place(g, ry, rx, product(g, ry, rx))
        wide.send(g, k)

        @pl.when(g == 0)
        def _():
            if k == 0:
                c_copy(last).wait()
            for ry, rx in NEW_BLOCKS[k]:
                tile = product(last, ry, rx)
                zt[ry, rx, 0] = tile[:own]
                zt[ry, rx, 1] = tile[own:]
                c_zx(ry, rx).start()

    def products_last(g, k):
        for ry, rx in NEW_BLOCKS[k]:
            c_zx(ry, rx).wait_recv()
            thin.place(0, ry, rx, plus(zt[ry, rx, zhi], zr[ry, rx]).astype(BF))
        thin.send(0, k)

    def second_sum(g):
        for h in range(2):
            wsum[h, g] = jnp.concatenate(wide.second_sum(h, g), axis=0).astype(BF)
        c_z(g).start()

    def powers(g):
        row = lax.broadcasted_iota(jnp.int32, (exps.shape[0], GW), 0)
        col = lax.broadcasted_iota(jnp.int32, (exps.shape[0], GW), 1)
        pick = jnp.where(row == g * (GW // 128) + col // 128, 1.0, 0.0).astype(BF)
        return lax.dot_general(
            exps[...].astype(F32).astype(BF), pick, (((0,), (0,)), ((), ())), preferred_element_type=F32)

    def adamw(g, grad):
        at = cols(g)
        first = (0.9 * f_v[:, at].astype(F32) + 0.1 * grad).astype(BF)
        second = (0.95 * s_v[:, at].astype(F32) + 0.05 * grad * grad).astype(BF)
        old = w_v[:, at].astype(F32)
        update = first.astype(F32) / (jnp.sqrt(second.astype(F32)) + 1e-08)
        fresh = (old - 0.1 * (update + 0.01 * old)).astype(BF)
        fo_v[:, at] = first
        so_v[:, at] = second
        wo_v[:, at] = fresh
        gap = anc_v[:, at].astype(F32) - fresh.astype(F32)
        packs[g, rep] = jnp.clip(gap * jnp.exp2(-powers(g)), -4.0, 4.0).astype(BF)
        for i in range(REPS - 1):
            c_pack(g, i).start()
        for copy in inner_outs(g):
            copy.start()

    def inner(g):
        c_z(g).wait_recv()
        @pl.when(g == 0)
        def _():
            for copy in ins:
                copy.wait()
        adamw(g, plus(wsum[zhi, g], rz[g]))

    def inner_last(g):
        adamw(last, jnp.concatenate(thin.second_sum(0, 0) + thin.second_sum(1, 0), axis=0))

    def outer(g):
        for i in range(REPS - 1):
            c_pack(g, i).wait_recv()
        at = cols(g)
        total = plus(*[packs[g, i] for i in range(REPS)])
        step = (jnp.exp2(powers(g)) * total) / REPS
        momentum = 0.9 * mom_v[:, at] + step
        mo_v[:, at] = momentum
        ao_v[:, at] = (anc_v[:, at].astype(F32) - 0.7 * (step + 0.9 * momentum)).astype(BF)
        for copy in outer_outs(g):
            copy.start()

    c_copy(0).start()
    for k in range(4):
        for ry, rx in NEW_BLOCKS[k]:
            a_copy(((y + OFFS[ry]) % RING) * RING + (x + OFFS[rx]) % RING).start()
        if k == 0:
            c_copy(last).start()
    for g in range(1, last):
        c_copy(g).start()
    for copy in ins:
        copy.start()

    everyone = [xp, xm, yp, ym, zdev] + mates
    barrier = pltpu.get_barrier_semaphore()
    for to in everyone:
        pl.semaphore_signal(barrier, inc=1, device_id=to, device_id_type=MESH)
    pl.semaphore_wait(barrier, len(everyone))

    def at_step(g, k, shift, stage, stage_last, only=None):
        group, kk = g + (k + shift) // 4, (k + shift) % 4
        if only is None or kk == only:
            rest = (kk,) if only is None else ()

            @pl.when(jnp.logical_and(group >= 0, group < last))
            def _():
                stage(group, *rest)

            if stage_last is not None:
                @pl.when(group == last)
                def _():
                    stage_last(0 if stage_last is not outer else group, *rest)

    first_turn = -((LEAD + 3) // 4)
    last_turn = -(-(LAGS[-1] + 3 + 1) // 4)

    @pl.loop(0, groups - first_turn + last_turn - 1)
    def _(turn):
        g = turn + first_turn
        for k in range(4):
            at_step(g, k, LEAD, products, products_last)
            at_step(g, k, FLEAD, wide.forward, thin.forward)
            at_step(g, k, 0, wide.first_sum, thin.first_sum)
            at_step(g, k, -LAGS[0], wide.forward2, thin.forward2, only=3)
            at_step(g, k, -LAGS[1], second_sum, None, only=3)
            at_step(g, k, -LAGS[2], inner, inner_last, only=3)
            at_step(g, k, -LAGS[3], outer, outer, only=3)

    @pl.loop(0, last)
    def _(g):
        wide.drain(g)
        c_z(g).wait_send()

    thin.drain(0)
    for ry in range(RING):
        for rx in range(RING):
            c_zx(ry, rx).wait_send()

    @pl.loop(0, groups)
    def _(g):
        for i in range(REPS - 1):
            c_pack(g, i).wait_send()
        for copy in inner_outs(g) + outer_outs(g):
            copy.wait()


def finish(*refs):
    sem = refs[-1]
    copies = [pltpu.make_async_copy(refs[i], refs[5 + i], sem.at[i]) for i in range(5)]
    for copy in copies:
        copy.start()
    for copy in copies:
        copy.wait()


def local(activations, cotangent, weight, first_moment, second_moment, anchor, momentum, exponents):
    own, width = anchor.shape
    tokens, rows = activations.shape[1:]
    groups = width // GW
    dma = pltpu.SemaphoreType.DMA
    anywhere = pl.BlockSpec(memory_space=pl.ANY)

    def buf(*shape, kind=BF):
        return pltpu.VMEM(shape, kind)

    def rings(count, unit):
        return [
            buf(2, count, RING, 8, unit, GW),
            buf(2, count, RING, 2, unit, GW), buf(2, count, RING, 2, unit, GW),
            buf(2, count, RING, unit, GW), buf(2, count, RING, unit, GW),
            buf(2, count, 8, unit, GW),
            buf(2, count, 2, unit, GW), buf(2, count, 2, unit, GW),
            buf(2, count, unit, GW), buf(2, count, unit, GW),
        ] + [dma((2, count, RING))] * 8 + [dma((2, count))] * 8

    outs = pl.pallas_call(
        kernel,
        out_shape=(
            jax.ShapeDtypeStruct(weight.shape, BF),
            jax.ShapeDtypeStruct(weight.shape, BF),
            jax.ShapeDtypeStruct(weight.shape, BF),
            jax.ShapeDtypeStruct(anchor.shape, BF),
            jax.ShapeDtypeStruct(momentum.shape, F32),
        ),
        in_specs=[anywhere] * 7 + [pl.BlockSpec(memory_space=pltpu.VMEM)],
        out_specs=[anywhere] * 5,
        scratch_shapes=[
            buf(tokens, rows), buf(tokens, width),
            buf(own, width), buf(own, width), buf(own, width), buf(own, width), buf(own, width, kind=F32),
            buf(own, width), buf(own, width), buf(own, width), buf(own, width), buf(own, width, kind=F32),
            buf(2, groups - 1, own, GW), buf(groups - 1, own, GW),
            buf(RING, RING, 2, own, GW), buf(RING, RING, own, GW), buf(groups, REPS, own, GW),
            dma((RING * RING,)), dma((groups,)), dma((5,)), dma((5, groups)),
            dma((groups - 1,)), dma((groups - 1,)), dma((RING, RING)), dma((RING, RING)),
            dma((groups, REPS - 1)), dma((groups, REPS - 1)),
        ] + rings(groups - 1, own // 2) + rings(1, own // 4),
        compiler_params=pltpu.CompilerParams(
            collective_id=0, has_side_effects=True, vmem_limit_bytes=58 * 1024 * 1024),
        cost_estimate=pl.CostEstimate(
            flops=2 * tokens * rows * width, bytes_accessed=12 * 2 ** 20, transcendentals=0),
        name="diloco_step",
    )(activations, cotangent, weight, first_moment, second_moment, anchor, momentum, exponents.T)
    return pl.pallas_call(
        finish,
        out_shape=[jax.ShapeDtypeStruct(o.shape, o.dtype) for o in outs],
        in_specs=[pl.BlockSpec(memory_space=pltpu.VMEM)] * 5,
        out_specs=[anywhere] * 5,
        scratch_shapes=[dma((5,))],
        name="results",
    )(*outs)


def solution(mesh):
    split = P("rep", "fsdp", None)
    rows = P("fsdp", None)
    return jax.shard_map(
        local,
        mesh=mesh,
        in_specs=(split, split, split, split, split, rows, rows, rows),
        out_specs=(split, split, split, rows, rows),
        check_vma=False,
    )
```

```python
import jax
import jax.numpy as jnp
from jax import lax
from jax.experimental import pallas as pl
from jax.experimental.pallas import tpu as pltpu
from jax.sharding import PartitionSpec as P

MESH = pl.DeviceIdType.MESH
BF = jnp.bfloat16
F32 = jnp.float32

RING = 4
REPS = 4
GW = 256
LEADS = (4, 4)
FLEADS = (2, 2)
LAGS = (1, 3, 5, 6, 7)
LAST_LAGS = (1, 2, 3, 4)
EXCHANGE = -3
OFFS = (2, 1, 3, 0)
A_SLOT = (0, 4, 2, 6)
B_SLOT = (3, 1, 5, 7)
NEW_BLOCKS = (
    ((0, 0), (0, 1), (0, 2), (1, 0), (2, 0)),
    ((1, 1), (1, 2), (2, 1)),
    ((2, 2), (0, 3), (3, 0)),
    ((3, 1), (3, 2), (1, 3), (2, 3), (3, 3)),
)
SEND_AFTER = ((3, 5), (2, 3), (1, 1), (2, 4))
FLAT = sum(NEW_BLOCKS, ())
BATCHES = tuple(FLAT[i:i + 2] for i in range(0, 16, 2))


def plus(*terms):
    total = terms[0].astype(F32)
    for term in terms[1:]:
        total = total + term.astype(F32)
    return total


class Rings:
    def __init__(self, refs, up, down, remote):
        (self.part, self.rp, self.rm, self.fp, self.fm, self.part2, self.rp2, self.rm2, self.fp2, self.fm2) = refs[:10]
        self.sems = refs[10:]
        self.up, self.down, self.remote = up, down, remote
        self.unit = self.part.shape[-2]

    def copy(self, which, h, g, k):
        part, sems = self.part, self.sems
        if which < 4:
            at, up, down = (h, g, k), self.up[h], self.down[h]
            rp, rm, fp, fm = self.rp, self.rm, self.fp, self.fm
        else:
            part, at, up, down = self.part2, (h, g), self.up[1 - h], self.down[1 - h]
            rp, rm, fp, fm = self.rp2, self.rm2, self.fp2, self.fm2
        src, dst, to = (
            (part.at[(*at, pl.ds(0, 2))], rp.at[at], up),
            (part.at[(*at, pl.ds(2, 2))], rm.at[at], down),
            (rp.at[(*at, 0)], fp.at[at], up),
            (rm.at[(*at, 1)], fm.at[at], down),
        )[which % 4]
        return self.remote(src, dst, sems[2 * which].at[at], sems[2 * which + 1].at[at], to)

    def place(self, g, ry, rx, tile):
        u = self.unit
        self.part[0, g, ry, A_SLOT[rx]] = tile[:u]
        self.part[0, g, ry, B_SLOT[rx]] = tile[u:2 * u]
        self.part[1, g, rx, A_SLOT[ry]] = tile[2 * u:3 * u]
        self.part[1, g, rx, B_SLOT[ry]] = tile[3 * u:]

    def send(self, h, g, k):
        self.copy(0, h, g, k).start()
        self.copy(1, h, g, k).start()

    def forward(self, g, k):
        for h in range(2):
            self.copy(0, h, g, k).wait_recv()
            self.rp[h, g, k, 0] = plus(self.rp[h, g, k, 0], self.part[h, g, k, 4]).astype(BF)
            self.copy(2, h, g, k).start()
            self.copy(1, h, g, k).wait_recv()
            self.rm[h, g, k, 1] = plus(self.rm[h, g, k, 1], self.part[h, g, k, 5]).astype(BF)
            self.copy(3, h, g, k).start()

    def first_sum(self, g, k):
        for h in range(2):
            self.copy(2, h, g, k).wait_recv()
            self.copy(3, h, g, k).wait_recv()
            self.part2[h, g, A_SLOT[k]] = plus(
                self.part[h, g, k, 6], self.fp[h, g, k], self.rm[h, g, k, 0]).astype(BF)
            self.part2[h, g, B_SLOT[k]] = plus(
                self.part[h, g, k, 7], self.fm[h, g, k], self.rp[h, g, k, 1]).astype(BF)
            if k == 2:
                self.copy(4, h, g, 0).start()
                self.copy(5, h, g, 0).start()

    def forward2(self, g):
        for h in range(2):
            self.copy(4, h, g, 0).wait_recv()
            self.rp2[h, g, 0] = plus(self.rp2[h, g, 0], self.part2[h, g, 4]).astype(BF)
            self.copy(6, h, g, 0).start()
            self.copy(5, h, g, 0).wait_recv()
            self.rm2[h, g, 1] = plus(self.rm2[h, g, 1], self.part2[h, g, 5]).astype(BF)
            self.copy(7, h, g, 0).start()

    def second_sum(self, h, g):
        self.copy(6, h, g, 0).wait_recv()
        self.copy(7, h, g, 0).wait_recv()
        return [
            plus(self.part2[h, g, 6], self.fp2[h, g], self.rm2[h, g, 0]),
            plus(self.part2[h, g, 7], self.fm2[h, g], self.rp2[h, g, 1]),
        ]

    def drain(self, g):
        for h in range(2):
            for k in range(RING):
                for which in range(4):
                    self.copy(which, h, g, k).wait_send()
            for which in range(4, 8):
                self.copy(which, h, g, 0).wait_send()


def kernel(act, cot, weight, first_in, second_in, anchor_in, mom_in, exps,
           w_out, f_out, s_out, anc_out, mom_out,
           a_v, c_v, w_v, f_v, s_v, anc_v, mom_v, wo_v, fo_v, so_v, ao_v, mo_v,
           wsum, rz, zt, zr, packs, pairs,
           a_sem, c_sem, in_sem, out_sem, z_s, z_r, zx_s, zx_r, k_s, k_r, *ring_refs):
    groups = c_v.shape[1] // GW
    last = groups - 1
    own = w_v.shape[0]
    block = 2 * own
    rep = lax.axis_index("rep")
    f = lax.axis_index("fsdp")
    zhi, x, y = f % 2, (f // 2) % RING, f // (2 * RING)

    def dev(x=x, y=y, zhi=zhi, rep=rep):
        return (rep, (y * RING + x) * 2 + zhi)

    xp, xm = dev(x=(x + 1) % RING), dev(x=(x + RING - 1) % RING)
    yp, ym = dev(y=(y + 1) % RING), dev(y=(y + RING - 1) % RING)
    zdev = dev(zhi=1 - zhi)
    zlo, core = rep // 2, rep % 2
    mate = dev(rep=2 * zlo + 1 - core)
    across = dev(rep=2 * (1 - zlo) + core), dev(rep=2 * (1 - zlo) + 1 - core)

    def cols(g):
        return pl.ds(pl.multiple_of(g * GW, GW), GW)

    def a_copy(blk):
        at = pl.ds(pl.multiple_of(blk * block, block), block)
        return pltpu.make_async_copy(act.at[0, :, at], a_v.at[:, at], a_sem.at[blk])

    def c_copy(g):
        return pltpu.make_async_copy(cot.at[0, :, cols(g)], c_v.at[:, cols(g)], c_sem.at[g])

    ins = [
        pltpu.make_async_copy(src, dst, in_sem.at[i])
        for i, (src, dst) in enumerate((
            (weight.at[0], w_v), (first_in.at[0], f_v), (second_in.at[0], s_v), (anchor_in, anc_v), (mom_in, mom_v)))
    ]

    def inner_outs(g):
        return [
            pltpu.make_async_copy(src.at[:, cols(g)], dst.at[0, :, cols(g)], out_sem.at[i, g])
            for i, (src, dst) in enumerate(((wo_v, w_out), (fo_v, f_out), (so_v, s_out)))
        ]

    def outer_outs(g):
        return [
            pltpu.make_async_copy(src.at[:, cols(g)], dst.at[:, cols(g)], out_sem.at[3 + i, g])
            for i, (src, dst) in enumerate(((ao_v, anc_out), (mo_v, mom_out)))
        ]

    def remote(src, dst, s, r, to):
        return pltpu.make_async_remote_copy(
            src_ref=src, dst_ref=dst, send_sem=s, recv_sem=r, device_id=to, device_id_type=MESH)

    def c_z(g):
        return remote(wsum.at[1 - zhi, g], rz.at[g], z_s.at[g], z_r.at[g], zdev)

    def c_zx(ry, rx):
        return remote(zt.at[ry, rx, 1 - zhi], zr.at[ry, rx], zx_s.at[ry, rx], zx_r.at[ry, rx], zdev)

    def c_pack(g):
        return remote(packs.at[g, core], packs.at[g, core], k_s.at[g, 0], k_r.at[g, 0], mate)

    def c_pair(g, i):
        here = pairs.at[g, zlo, core]
        return remote(here, here, k_s.at[g, 1 + i], k_r.at[g, 1 + i], across[i])

    wide = Rings(ring_refs[:26], (xp, yp), (xm, ym), remote)
    thin = Rings(ring_refs[26:], (xp, yp), (xm, ym), remote)

    def product(g, ry, rx):
        blk = ((y + OFFS[ry]) % RING) * RING + (x + OFFS[rx]) % RING
        at = pl.ds(pl.multiple_of(blk * block, block), block)
        return lax.dot_general(
            a_v[:, at], c_v[:, cols(g)], (((0,), (0,)), ((), ())), preferred_element_type=F32).astype(BF)

    def products(g, k):
        @pl.when(g == 0)
        def _():
            for ry, rx in NEW_BLOCKS[k]:
                a_copy(((y + OFFS[ry]) % RING) * RING + (x + OFFS[rx]) % RING).wait()

        if k == 0:
            c_copy(g).wait()
        for n, (ry, rx) in enumerate(NEW_BLOCKS[k]):
            wide.place(g, ry, rx, product(g, ry, rx))
            for h in range(2):
                if n + 1 == SEND_AFTER[k][h]:
                    if k == 0 and h == 0:
                        @pl.when(g == 0)
                        def _():
                            pl.semaphore_wait(barrier, len(everyone))
                    wide.send(h, g, k)
        if k == 0:
            @pl.when(g == 0)
            def _():
                load_rest()

    def exchange(n):
        if n == 0:
            c_copy(last).wait()
        for ry, rx in BATCHES[n]:
            tile = product(last, ry, rx)
            zt[ry, rx, 0] = tile[:own]
            zt[ry, rx, 1] = tile[own:]
            c_zx(ry, rx).start()

    def products_last(g, k):
        for n, (ry, rx) in enumerate(NEW_BLOCKS[k]):
            c_zx(ry, rx).wait_recv()
            thin.place(0, ry, rx, plus(zt[ry, rx, zhi], zr[ry, rx]).astype(BF))
            for h in range(2):
                if n + 1 == SEND_AFTER[k][h]:
                    thin.send(h, 0, k)

    def second_sum(g):
        for h in range(2):
            wsum[h, g] = jnp.concatenate(wide.second_sum(h, g), axis=0).astype(BF)
        c_z(g).start()

    def powers(g):
        row = lax.broadcasted_iota(jnp.int32, (exps.shape[0], GW), 0)
        col = lax.broadcasted_iota(jnp.int32, (exps.shape[0], GW), 1)
        pick = jnp.where(row == g * (GW // 128) + col // 128, 1.0, 0.0).astype(BF)
        return lax.dot_general(
            exps[...].astype(F32).astype(BF), pick, (((0,), (0,)), ((), ())), preferred_element_type=F32)

    def adamw(g, grad):
        at = cols(g)
        first = (0.9 * f_v[:, at].astype(F32) + 0.1 * grad).astype(BF)
        second = (0.95 * s_v[:, at].astype(F32) + 0.05 * grad * grad).astype(BF)
        old = w_v[:, at].astype(F32)
        update = first.astype(F32) / (jnp.sqrt(second.astype(F32)) + 1e-08)
        fresh = (old - 0.1 * (update + 0.01 * old)).astype(BF)
        fo_v[:, at] = first
        so_v[:, at] = second
        wo_v[:, at] = fresh
        gap = anc_v[:, at].astype(F32) - fresh.astype(F32)
        packs[g, core] = jnp.clip(gap * jnp.exp2(-powers(g)), -4.0, 4.0).astype(BF)
        c_pack(g).start()
        for copy in inner_outs(g):
            copy.start()

    def inner(g):
        c_z(g).wait_recv()
        @pl.when(g == 0)
        def _():
            for copy in ins:
                copy.wait()
        adamw(g, plus(wsum[zhi, g], rz[g]))

    def thin_forward(g, k):
        thin.forward(0, k)

    def thin_first_sum(g, k):
        thin.first_sum(0, k)

    def thin_forward2(g):
        thin.forward2(0)

    def inner_last(g):
        adamw(last, jnp.concatenate(thin.second_sum(0, 0) + thin.second_sum(1, 0), axis=0))

    def pair(g):
        c_pack(g).wait_recv()
        both = plus(packs[g, 0], packs[g, 1]).astype(BF)
        pairs[g, zlo, 0] = both[:own // 2]
        pairs[g, zlo, 1] = both[own // 2:]
        for i in range(2):
            c_pair(g, i).start()

    def outer(g):
        for i in range(2):
            c_pair(g, i).wait_recv()
        at = cols(g)
        total = jnp.concatenate([plus(pairs[g, 0, i], pairs[g, 1, i]) for i in range(2)], axis=0)
        step = (jnp.exp2(powers(g)) * total) / REPS
        momentum = 0.9 * mom_v[:, at] + step
        mo_v[:, at] = momentum
        ao_v[:, at] = (anc_v[:, at].astype(F32) - 0.7 * (step + 0.9 * momentum)).astype(BF)
        for copy in outer_outs(g):
            copy.start()

    everyone = [xp, xm, yp, ym, zdev, mate, *across]
    barrier = pltpu.get_barrier_semaphore()
    for to in everyone:
        pl.semaphore_signal(barrier, inc=1, device_id=to, device_id_type=MESH)

    def load(k):
        for ry, rx in NEW_BLOCKS[k]:
            a_copy(((y + OFFS[ry]) % RING) * RING + (x + OFFS[rx]) % RING).start()

    def load_rest():
        for k in range(1, RING):
            load(k)
        for g in (last, *range(1, last)):
            c_copy(g).start()
        for copy in ins:
            copy.start()

    c_copy(0).start()
    load(0)

    def at_step(g, k, shift, stage, groups_of, *late):
        group, kk = g + (k + shift) // RING, (k + shift) % RING
        if not late or kk == RING - 1:
            @pl.when(groups_of(group))
            def _():
                stage(group) if late else stage(group, kk)

    def is_wide(group):
        return jnp.logical_and(group >= 0, group < last)

    def is_last(group):
        return group == last

    first_turn = -((max(LEADS) + RING - 1) // RING)
    end = max(LAGS[-1] - RING, LAST_LAGS[-1])
    last_turn = -(-(end + RING) // RING)

    @pl.loop(0, groups - first_turn + last_turn - 1)
    def _(turn):
        g = turn + first_turn
        for k in range(RING):
            at_step(g, k, LEADS[0], products, is_wide)
            at_step(g, k, LEADS[1], products_last, is_last)
            for n in range(len(BATCHES)):
                step = n + EXCHANGE
                if step % RING == k:
                    @pl.when(g == step // RING)
                    def _():
                        exchange(n)

            at_step(g, k, FLEADS[0], wide.forward, is_wide)
            at_step(g, k, FLEADS[1], thin_forward, is_last)
            at_step(g, k, 0, wide.first_sum, is_wide)
            at_step(g, k, 0, thin_first_sum, is_last)
            for lag, stage in zip(LAST_LAGS, (thin_forward2, inner_last, pair, outer)):
                at_step(g, k, -lag, stage, is_last, "late")
            for lag, stage in zip(LAGS, (wide.forward2, second_sum, inner, pair, outer)):
                at_step(g, k, -lag, stage, is_wide, "late")

    @pl.loop(0, last)
    def _(g):
        wide.drain(g)
        c_z(g).wait_send()

    thin.drain(0)
    for ry in range(RING):
        for rx in range(RING):
            c_zx(ry, rx).wait_send()

    @pl.loop(0, groups)
    def _(g):
        c_pack(g).wait_send()
        for i in range(2):
            c_pair(g, i).wait_send()
        for copy in inner_outs(g) + outer_outs(g):
            copy.wait()


def finish(*refs):
    given, made, held = refs[:5], refs[5:10], refs[10:15]
    sem = refs[15]
    inward = [pltpu.make_async_copy(given[i], held[i], sem.at[0, i]) for i in range(5)]
    outward = [pltpu.make_async_copy(held[i], made[i], sem.at[1, i]) for i in range(5)]
    for copy in inward:
        copy.start()
    for arrived, copy in zip(inward, outward):
        arrived.wait()
        copy.start()
    for copy in outward:
        copy.wait()


def local(activations, cotangent, weight, first_moment, second_moment, anchor, momentum, exponents):
    own, width = anchor.shape
    tokens, rows = activations.shape[1:]
    groups = width // GW
    dma = pltpu.SemaphoreType.DMA
    anywhere = pl.BlockSpec(memory_space=pl.ANY)

    def buf(*shape, kind=BF):
        return pltpu.VMEM(shape, kind)

    def rings(count, unit):
        return [
            buf(2, count, RING, 8, unit, GW),
            buf(2, count, RING, 2, unit, GW), buf(2, count, RING, 2, unit, GW),
            buf(2, count, RING, unit, GW), buf(2, count, RING, unit, GW),
            buf(2, count, 8, unit, GW),
            buf(2, count, 2, unit, GW), buf(2, count, 2, unit, GW),
            buf(2, count, unit, GW), buf(2, count, unit, GW),
        ] + [dma((2, count, RING))] * 8 + [dma((2, count))] * 8

    outs = pl.pallas_call(
        kernel,
        out_shape=(
            jax.ShapeDtypeStruct(weight.shape, BF),
            jax.ShapeDtypeStruct(weight.shape, BF),
            jax.ShapeDtypeStruct(weight.shape, BF),
            jax.ShapeDtypeStruct(anchor.shape, BF),
            jax.ShapeDtypeStruct(momentum.shape, F32),
        ),
        in_specs=[anywhere] * 7 + [pl.BlockSpec(memory_space=pltpu.VMEM)],
        out_specs=[anywhere] * 5,
        scratch_shapes=[
            buf(tokens, rows), buf(tokens, width),
            buf(own, width), buf(own, width), buf(own, width), buf(own, width), buf(own, width, kind=F32),
            buf(own, width), buf(own, width), buf(own, width), buf(own, width), buf(own, width, kind=F32),
            buf(2, groups - 1, own, GW), buf(groups - 1, own, GW),
            buf(RING, RING, 2, own, GW), buf(RING, RING, own, GW),
            buf(groups, 2, own, GW), buf(groups, 2, 2, own // 2, GW),
            dma((RING * RING,)), dma((groups,)), dma((5,)), dma((5, groups)),
            dma((groups - 1,)), dma((groups - 1,)), dma((RING, RING)), dma((RING, RING)),
            dma((groups, 3)), dma((groups, 3)),
        ] + rings(groups - 1, own // 2) + rings(1, own // 4),
        compiler_params=pltpu.CompilerParams(
            collective_id=0, has_side_effects=True, vmem_limit_bytes=58 * 1024 * 1024),
        cost_estimate=pl.CostEstimate(
            flops=2 * tokens * rows * width, bytes_accessed=12 * 2 ** 20, transcendentals=0),
        name="diloco_step",
    )(activations, cotangent, weight, first_moment, second_moment, anchor, momentum, exponents.T)
    return pl.pallas_call(
        finish,
        out_shape=[jax.ShapeDtypeStruct(o.shape, o.dtype) for o in outs],
        in_specs=[anywhere] * 5,
        out_specs=[anywhere] * 5,
        scratch_shapes=[buf(*o.shape, kind=o.dtype) for o in outs] + [dma((2, 5))],
        name="results",
    )(*outs)


def solution(mesh):
    split = P("rep", "fsdp", None)
    rows = P("fsdp", None)
    return jax.shard_map(
        local,
        mesh=mesh,
        in_specs=(split, split, split, split, split, rows, rows, rows),
        out_specs=(split, split, split, rows, rows),
        check_vma=False,
    )
```

```python
import jax
import jax.numpy as jnp
from jax import lax
from jax.experimental import pallas as pl
from jax.experimental.pallas import tpu as pltpu
from jax.sharding import PartitionSpec as P

MESH = pl.DeviceIdType.MESH
BF = jnp.bfloat16
F32 = jnp.float32

RING = 4
REPS = 4
GW = 256
LEADS = (4, 4)
FLEADS = (2, 2)
LAGS = (1, 3, 5, 6, 7, 7)
END = ((0, "forward"), (1, "sum"), (3, "inner_last"), (3, "inner"), (4, "pair_last"), (4, "pair"), (4, "tidy_last"), (4, "tidy"), (4, "outer_last"), (4, "outer"))
EXCHANGE = -3
OFFS = (2, 1, 3, 0)
A_SLOT = (0, 4, 2, 6)
B_SLOT = (3, 1, 5, 7)
NEW_BLOCKS = (
    ((0, 0), (0, 1), (0, 2), (1, 0), (2, 0)),
    ((1, 1), (1, 2), (2, 1)),
    ((2, 2), (0, 3), (3, 0)),
    ((3, 1), (3, 2), (1, 3), (2, 3), (3, 3)),
)
SEND_AFTER = ((3, 5), (2, 3), (1, 1), (2, 4))
FLAT = sum(NEW_BLOCKS, ())
BATCHES = tuple(FLAT[i:i + 2] for i in range(0, 16, 2))


def plus(*terms):
    total = terms[0].astype(F32)
    for term in terms[1:]:
        total = total + term.astype(F32)
    return total


class Rings:
    def __init__(self, refs, up, down, remote):
        (self.part, self.rp, self.rm, self.fp, self.fm, self.part2, self.rp2, self.rm2, self.fp2, self.fm2) = refs[:10]
        self.sems = refs[10:]
        self.up, self.down, self.remote = up, down, remote
        self.unit = self.part.shape[-2]

    def copy(self, which, h, g, k):
        part, sems = self.part, self.sems
        if which < 4:
            at, up, down = (h, g, k), self.up[h], self.down[h]
            rp, rm, fp, fm = self.rp, self.rm, self.fp, self.fm
        else:
            part, at, up, down = self.part2, (h, g), self.up[1 - h], self.down[1 - h]
            rp, rm, fp, fm = self.rp2, self.rm2, self.fp2, self.fm2
        src, dst, to = (
            (part.at[(*at, pl.ds(0, 2))], rp.at[at], up),
            (part.at[(*at, pl.ds(2, 2))], rm.at[at], down),
            (rp.at[(*at, 0)], fp.at[at], up),
            (rm.at[(*at, 1)], fm.at[at], down),
        )[which % 4]
        return self.remote(src, dst, sems[2 * which].at[at], sems[2 * which + 1].at[at], to)

    def place(self, g, ry, rx, tile):
        u = self.unit
        self.part[0, g, ry, A_SLOT[rx]] = tile[:u]
        self.part[0, g, ry, B_SLOT[rx]] = tile[u:2 * u]
        self.part[1, g, rx, A_SLOT[ry]] = tile[2 * u:3 * u]
        self.part[1, g, rx, B_SLOT[ry]] = tile[3 * u:]

    def send(self, h, g, k):
        self.copy(0, h, g, k).start()
        self.copy(1, h, g, k).start()

    def forward(self, g, k):
        for h in range(2):
            self.copy(0, h, g, k).wait_recv()
            self.rp[h, g, k, 0] = plus(self.rp[h, g, k, 0], self.part[h, g, k, 4]).astype(BF)
            self.copy(2, h, g, k).start()
            self.copy(1, h, g, k).wait_recv()
            self.rm[h, g, k, 1] = plus(self.rm[h, g, k, 1], self.part[h, g, k, 5]).astype(BF)
            self.copy(3, h, g, k).start()

    def first_sum(self, g, k):
        for h in range(2):
            self.copy(2, h, g, k).wait_recv()
            self.copy(3, h, g, k).wait_recv()
            self.part2[h, g, A_SLOT[k]] = plus(
                self.part[h, g, k, 6], self.fp[h, g, k], self.rm[h, g, k, 0]).astype(BF)
            self.part2[h, g, B_SLOT[k]] = plus(
                self.part[h, g, k, 7], self.fm[h, g, k], self.rp[h, g, k, 1]).astype(BF)
            if k == 2:
                self.copy(4, h, g, 0).start()
                self.copy(5, h, g, 0).start()

    def forward2(self, g):
        for h in range(2):
            self.copy(4, h, g, 0).wait_recv()
            self.rp2[h, g, 0] = plus(self.rp2[h, g, 0], self.part2[h, g, 4]).astype(BF)
            self.copy(6, h, g, 0).start()
            self.copy(5, h, g, 0).wait_recv()
            self.rm2[h, g, 1] = plus(self.rm2[h, g, 1], self.part2[h, g, 5]).astype(BF)
            self.copy(7, h, g, 0).start()

    def second_sum(self, h, g):
        self.copy(6, h, g, 0).wait_recv()
        self.copy(7, h, g, 0).wait_recv()
        return [
            plus(self.part2[h, g, 6], self.fp2[h, g], self.rm2[h, g, 0]),
            plus(self.part2[h, g, 7], self.fm2[h, g], self.rp2[h, g, 1]),
        ]

    def drain(self, g):
        for h in range(2):
            for k in range(RING):
                for which in range(4):
                    self.copy(which, h, g, k).wait_send()
            for which in range(4, 8):
                self.copy(which, h, g, 0).wait_send()


class ShortRings(Rings):
    def __init__(self, refs, up, down, owners, remote):
        self.part, self.rp, self.rm, self.fp, self.fm, self.part2, self.got = refs[:7]
        self.sems, self.q_s, self.q_r = refs[7:15], refs[15], refs[16]
        self.up, self.down, self.owners, self.remote = up, down, owners, remote
        self.unit = self.part.shape[-2]

    def straight(self, h, k):
        return self.remote(
            self.part2.at[h, k], self.got.at[h, k], self.q_s.at[h, k], self.q_r.at[h, k], self.owners[1 - h][k])

    def first_sum(self, g, k):
        for h in range(2):
            self.copy(2, h, g, k).wait_recv()
            self.copy(3, h, g, k).wait_recv()
            self.part2[h, k, 0] = plus(self.part[h, g, k, 6], self.fp[h, g, k], self.rm[h, g, k, 0]).astype(BF)
            self.part2[h, k, 1] = plus(self.part[h, g, k, 7], self.fm[h, g, k], self.rp[h, g, k, 1]).astype(BF)
            if k < 3:
                self.straight(h, k).start()

    def second_sum(self, h, g):
        for k in range(3):
            self.straight(h, k).wait_recv()
        return [plus(self.part2[h, 3, i], *[self.got[h, k, i] for k in range(3)]) for i in range(2)]

    def drain(self, g):
        for h in range(2):
            for k in range(RING):
                for which in range(4):
                    self.copy(which, h, g, k).wait_send()
            for k in range(3):
                self.straight(h, k).wait_send()


def kernel(act, cot, weight, first_in, second_in, anchor_in, mom_in, exps_in,
           w_out, f_out, s_out, anc_out, mom_out,
           a_v, c_v, w_v, f_v, s_v, anc_v, mom_v, wo_v, fo_v, so_v, ao_v, mo_v,
           exps, wsum, rz, zt, zr, packs, pairs,
           a_sem, c_sem, in_sem, out_sem, z_s, z_r, zx_s, zx_r, k_s, k_r, *ring_refs):
    groups = c_v.shape[1] // GW
    last = groups - 1
    own = w_v.shape[0]
    block = 2 * own
    rep = lax.axis_index("rep")
    f = lax.axis_index("fsdp")
    zhi, x, y = f % 2, (f // 2) % RING, f // (2 * RING)

    def dev(x=x, y=y, zhi=zhi, rep=rep):
        return (rep, (y * RING + x) * 2 + zhi)

    xp, xm = dev(x=(x + 1) % RING), dev(x=(x + RING - 1) % RING)
    yp, ym = dev(y=(y + 1) % RING), dev(y=(y + RING - 1) % RING)
    x2, y2 = dev(x=(x + 2) % RING), dev(y=(y + 2) % RING)
    zdev = dev(zhi=1 - zhi)
    zlo, core = rep // 2, rep % 2
    mate = dev(rep=2 * zlo + 1 - core)
    across = dev(rep=2 * (1 - zlo) + core), dev(rep=2 * (1 - zlo) + 1 - core)

    def cols(g):
        return pl.ds(pl.multiple_of(g * GW, GW), GW)

    def a_copy(blk):
        at = pl.ds(pl.multiple_of(blk * block, block), block)
        return pltpu.make_async_copy(act.at[0, :, at], a_v.at[:, at], a_sem.at[blk])

    def c_copy(g):
        return pltpu.make_async_copy(cot.at[0, :, cols(g)], c_v.at[:, cols(g)], c_sem.at[g])

    ins = [
        pltpu.make_async_copy(src, dst, in_sem.at[i])
        for i, (src, dst) in enumerate((
            (weight.at[0], w_v), (first_in.at[0], f_v), (second_in.at[0], s_v), (anchor_in, anc_v), (mom_in, mom_v),
            (exps_in, exps)))
    ]

    def inner_outs(g):
        return [
            pltpu.make_async_copy(src.at[:, cols(g)], dst.at[0, :, cols(g)], out_sem.at[i, g])
            for i, (src, dst) in enumerate(((wo_v, w_out), (fo_v, f_out), (so_v, s_out)))
        ]

    def outer_outs(g):
        return [
            pltpu.make_async_copy(src.at[:, cols(g)], dst.at[:, cols(g)], out_sem.at[3 + i, g])
            for i, (src, dst) in enumerate(((ao_v, anc_out), (mo_v, mom_out)))
        ]

    def remote(src, dst, s, r, to):
        return pltpu.make_async_remote_copy(
            src_ref=src, dst_ref=dst, send_sem=s, recv_sem=r, device_id=to, device_id_type=MESH)

    def c_z(g):
        return remote(wsum.at[1 - zhi, g], rz.at[g], z_s.at[g], z_r.at[g], zdev)

    def c_zx(ry, rx):
        return remote(zt.at[ry, rx, 1 - zhi], zr.at[ry, rx], zx_s.at[ry, rx], zx_r.at[ry, rx], zdev)

    def c_pack(g):
        return remote(packs.at[g, core], packs.at[g, core], k_s.at[g, 0], k_r.at[g, 0], mate)

    def c_pair(g, i):
        here = pairs.at[g, zlo, core]
        return remote(here, here, k_s.at[g, 1 + i], k_r.at[g, 1 + i], across[i])

    wide = Rings(ring_refs[:26], (xp, yp), (xm, ym), remote)
    thin = ShortRings(ring_refs[26:], (xp, yp), (xm, ym), ((x2, xp, xm), (y2, yp, ym)), remote)

    def product(g, ry, rx):
        blk = ((y + OFFS[ry]) % RING) * RING + (x + OFFS[rx]) % RING
        at = pl.ds(pl.multiple_of(blk * block, block), block)
        return lax.dot_general(
            a_v[:, at], c_v[:, cols(g)], (((0,), (0,)), ((), ())), preferred_element_type=F32).astype(BF)

    def products(g, k):
        @pl.when(g == 0)
        def _():
            for ry, rx in NEW_BLOCKS[k]:
                a_copy(((y + OFFS[ry]) % RING) * RING + (x + OFFS[rx]) % RING).wait()

        if k == 0:
            c_copy(g).wait()
        for n, (ry, rx) in enumerate(NEW_BLOCKS[k]):
            wide.place(g, ry, rx, product(g, ry, rx))
            for h in range(2):
                if n + 1 == SEND_AFTER[k][h]:
                    if k == 0 and h == 0:
                        @pl.when(g == 0)
                        def _():
                            pl.semaphore_wait(barrier, len(everyone))
                    wide.send(h, g, k)
        if k == 0:
            @pl.when(g == 0)
            def _():
                load_rest()

    def exchange(n):
        if n == 0:
            c_copy(last).wait()
        for ry, rx in BATCHES[n]:
            tile = product(last, ry, rx)
            zt[ry, rx, 0] = tile[:own]
            zt[ry, rx, 1] = tile[own:]
            c_zx(ry, rx).start()

    def products_last(g, k):
        for n, (ry, rx) in enumerate(NEW_BLOCKS[k]):
            c_zx(ry, rx).wait_recv()
            thin.place(0, ry, rx, plus(zt[ry, rx, zhi], zr[ry, rx]).astype(BF))
            for h in range(2):
                if n + 1 == SEND_AFTER[k][h]:
                    thin.send(h, 0, k)

    def second_sum(g):
        for h in range(2):
            wsum[h, g] = jnp.concatenate(wide.second_sum(h, g), axis=0).astype(BF)
        c_z(g).start()

    def powers(g):
        row = lax.broadcasted_iota(jnp.int32, (exps.shape[0], GW), 0)
        col = lax.broadcasted_iota(jnp.int32, (exps.shape[0], GW), 1)
        pick = jnp.where(row == g * (GW // 128) + col // 128, 1.0, 0.0).astype(BF)
        return lax.dot_general(
            exps[...].astype(F32).astype(BF), pick, (((0,), (0,)), ((), ())), preferred_element_type=F32)

    def adamw(g, grad):
        at = cols(g)
        first = (0.9 * f_v[:, at].astype(F32) + 0.1 * grad).astype(BF)
        second = (0.95 * s_v[:, at].astype(F32) + 0.05 * grad * grad).astype(BF)
        old = w_v[:, at].astype(F32)
        update = first.astype(F32) / (jnp.sqrt(second.astype(F32)) + 1e-08)
        fresh = (old - 0.1 * (update + 0.01 * old)).astype(BF)
        fo_v[:, at] = first
        so_v[:, at] = second
        wo_v[:, at] = fresh
        gap = anc_v[:, at].astype(F32) - fresh.astype(F32)
        packs[g, core] = jnp.clip(gap * jnp.exp2(-powers(g)), -4.0, 4.0).astype(BF)
        c_pack(g).start()
        for copy in inner_outs(g):
            copy.start()

    def inner(g):
        c_z(g).wait_recv()
        @pl.when(g == 0)
        def _():
            for copy in ins:
                copy.wait()
        adamw(g, plus(wsum[zhi, g], rz[g]))

    def thin_forward(g, k):
        thin.forward(0, k)

    def thin_first_sum(g, k):
        thin.first_sum(0, k)

    def inner_last(g):
        adamw(last, jnp.concatenate(thin.second_sum(0, 0) + thin.second_sum(1, 0), axis=0))

    def pair(g):
        c_pack(g).wait_recv()
        both = plus(packs[g, 0], packs[g, 1]).astype(BF)
        pairs[g, zlo, 0] = both[:own // 2]
        pairs[g, zlo, 1] = both[own // 2:]
        for i in range(2):
            c_pair(g, i).start()

    def outer(g):
        for i in range(2):
            c_pair(g, i).wait_recv()
        at = cols(g)
        total = jnp.concatenate([plus(pairs[g, 0, i], pairs[g, 1, i]) for i in range(2)], axis=0)
        step = (jnp.exp2(powers(g)) * total) / REPS
        momentum = 0.9 * mom_v[:, at] + step
        mo_v[:, at] = momentum
        ao_v[:, at] = (anc_v[:, at].astype(F32) - 0.7 * (step + 0.9 * momentum)).astype(BF)
        for copy in outer_outs(g):
            copy.start()

    def tidy(g):
        wide.drain(g)
        c_z(g).wait_send()
        c_pack(g).wait_send()
        for i in range(2):
            c_pair(g, i).wait_send()

    def tidy_last(g):
        thin.drain(0)
        for ry in range(RING):
            for rx in range(RING):
                c_zx(ry, rx).wait_send()
        c_pack(g).wait_send()
        for i in range(2):
            c_pair(g, i).wait_send()

    before = last - 1
    ends = dict(
        forward=lambda: wide.forward2(before), sum=lambda: second_sum(before), inner=lambda: inner(before),
        pair=lambda: pair(before), outer=lambda: outer(before), tidy=lambda: tidy(before),
        inner_last=lambda: inner_last(last), pair_last=lambda: pair(last), outer_last=lambda: outer(last),
        tidy_last=lambda: tidy_last(last))

    everyone = [xp, xm, x2, yp, ym, y2, zdev, mate, *across]
    barrier = pltpu.get_barrier_semaphore()
    for to in everyone:
        pl.semaphore_signal(barrier, inc=1, device_id=to, device_id_type=MESH)

    def load(k):
        for ry, rx in NEW_BLOCKS[k]:
            a_copy(((y + OFFS[ry]) % RING) * RING + (x + OFFS[rx]) % RING).start()

    def load_rest():
        for k in range(1, RING):
            load(k)
        for g in (last, *range(1, last)):
            c_copy(g).start()
        for copy in ins:
            copy.start()

    c_copy(0).start()
    load(0)

    def at_step(g, k, shift, stage, groups_of, *late):
        group, kk = g + (k + shift) // RING, (k + shift) % RING
        if not late or kk == RING - 1:
            @pl.when(groups_of(group))
            def _():
                stage(group) if late else stage(group, kk)

    def is_wide(group):
        return jnp.logical_and(group >= 0, group < last)

    def is_early(group):
        return jnp.logical_and(group >= 0, group < last - 1)

    def is_last(group):
        return group == last

    first_turn = -((max(LEADS) + RING - 1) // RING)
    last_turn = END[-1][0] // RING

    @pl.loop(0, groups - first_turn + last_turn)
    def _(turn):
        g = turn + first_turn
        for k in range(RING):
            at_step(g, k, LEADS[0], products, is_wide)
            at_step(g, k, LEADS[1], products_last, is_last)
            for n in range(len(BATCHES)):
                step = n + EXCHANGE
                if step % RING == k:
                    @pl.when(g == step // RING)
                    def _():
                        exchange(n)

            at_step(g, k, FLEADS[0], wide.forward, is_wide)
            at_step(g, k, FLEADS[1], thin_forward, is_last)
            at_step(g, k, 0, wide.first_sum, is_wide)
            at_step(g, k, 0, thin_first_sum, is_last)
            for lag, stage in zip(LAGS, (wide.forward2, second_sum, inner, pair, outer, tidy)):
                at_step(g, k, -lag, stage, is_early, "late")
            for step, stage in END:
                if step % RING == k:
                    @pl.when(g == last + step // RING)
                    def _():
                        ends[stage]()


    for g in range(groups):
        for copy in inner_outs(g) + outer_outs(g):
            copy.wait()


def finish(*refs):
    given, made, held = refs[:5], refs[5:10], refs[10:15]
    sem = refs[15]
    inward = [pltpu.make_async_copy(given[i], held[i], sem.at[0, i]) for i in range(5)]
    outward = [pltpu.make_async_copy(held[i], made[i], sem.at[1, i]) for i in range(5)]
    for copy in inward:
        copy.start()
    for arrived, copy in zip(inward, outward):
        arrived.wait()
        copy.start()
    for copy in outward:
        copy.wait()


def local(activations, cotangent, weight, first_moment, second_moment, anchor, momentum, exponents):
    own, width = anchor.shape
    tokens, rows = activations.shape[1:]
    groups = width // GW
    dma = pltpu.SemaphoreType.DMA
    anywhere = pl.BlockSpec(memory_space=pl.ANY)

    def buf(*shape, kind=BF):
        return pltpu.VMEM(shape, kind)

    def rings(count, unit):
        return [
            buf(2, count, RING, 8, unit, GW),
            buf(2, count, RING, 2, unit, GW), buf(2, count, RING, 2, unit, GW),
            buf(2, count, RING, unit, GW), buf(2, count, RING, unit, GW),
            buf(2, count, 8, unit, GW),
            buf(2, count, 2, unit, GW), buf(2, count, 2, unit, GW),
            buf(2, count, unit, GW), buf(2, count, unit, GW),
        ] + [dma((2, count, RING))] * 8 + [dma((2, count))] * 8

    def short_rings(unit):
        return [
            buf(2, 1, RING, 8, unit, GW),
            buf(2, 1, RING, 2, unit, GW), buf(2, 1, RING, 2, unit, GW),
            buf(2, 1, RING, unit, GW), buf(2, 1, RING, unit, GW),
            buf(2, RING, 2, unit, GW), buf(2, RING - 1, 2, unit, GW),
        ] + [dma((2, 1, RING))] * 8 + [dma((2, RING - 1))] * 2

    outs = pl.pallas_call(
        kernel,
        out_shape=(
            jax.ShapeDtypeStruct(weight.shape, BF),
            jax.ShapeDtypeStruct(weight.shape, BF),
            jax.ShapeDtypeStruct(weight.shape, BF),
            jax.ShapeDtypeStruct(anchor.shape, BF),
            jax.ShapeDtypeStruct(momentum.shape, F32),
        ),
        in_specs=[anywhere] * 8,
        out_specs=[anywhere] * 5,
        scratch_shapes=[
            buf(tokens, rows), buf(tokens, width),
            buf(own, width), buf(own, width), buf(own, width), buf(own, width), buf(own, width, kind=F32),
            buf(own, width), buf(own, width), buf(own, width), buf(own, width), buf(own, width, kind=F32),
            buf(*exponents.shape[::-1], kind=jnp.int32),
            buf(2, groups - 1, own, GW), buf(groups - 1, own, GW),
            buf(RING, RING, 2, own, GW), buf(RING, RING, own, GW),
            buf(groups, 2, own, GW), buf(groups, 2, 2, own // 2, GW),
            dma((RING * RING,)), dma((groups,)), dma((6,)), dma((5, groups)),
            dma((groups - 1,)), dma((groups - 1,)), dma((RING, RING)), dma((RING, RING)),
            dma((groups, 3)), dma((groups, 3)),
        ] + rings(groups - 1, own // 2) + short_rings(own // 4),
        compiler_params=pltpu.CompilerParams(
            collective_id=0, has_side_effects=True, vmem_limit_bytes=58 * 1024 * 1024),
        cost_estimate=pl.CostEstimate(
            flops=2 * tokens * rows * width, bytes_accessed=12 * 2 ** 20, transcendentals=0),
        name="diloco_step",
    )(activations, cotangent, weight, first_moment, second_moment, anchor, momentum, exponents.T)
    return pl.pallas_call(
        finish,
        out_shape=[jax.ShapeDtypeStruct(o.shape, o.dtype) for o in outs],
        in_specs=[anywhere] * 5,
        out_specs=[anywhere] * 5,
        scratch_shapes=[buf(*o.shape, kind=o.dtype) for o in outs] + [dma((2, 5))],
        name="results",
    )(*outs)


def solution(mesh):
    split = P("rep", "fsdp", None)
    rows = P("fsdp", None)
    return jax.shard_map(
        local,
        mesh=mesh,
        in_specs=(split, split, split, split, split, rows, rows, rows),
        out_specs=(split, split, split, rows, rows),
        check_vma=False,
    )
```

```python
import jax
import jax.numpy as jnp
from jax import lax
from jax.experimental import pallas as pl
from jax.experimental.pallas import tpu as pltpu
from jax.sharding import PartitionSpec as P

MESH = pl.DeviceIdType.MESH
BF = jnp.bfloat16
F32 = jnp.float32

RING = 4
REPS = 4
GW = 256
LEADS = (4, 4)
FLEADS = (2, 2)
LAGS = (1, 3, 5, 6, 7, 7, 7)
END = ((0, "forward"), (1, "sum"), (3, "inner_last"), (3, "inner"), (4, "pair_last"), (4, "pair"), (4, "tidy_last"), (4, "tidy"), (4, "share_last"), (4, "share"), (4, "outer_last"), (4, "outer"))
EXCHANGE = -3
OFFS = (2, 1, 3, 0)
A_SLOT = (0, 4, 2, 6)
B_SLOT = (3, 1, 5, 7)
NEW_BLOCKS = (
    ((0, 0), (0, 1), (0, 2), (1, 0), (2, 0)),
    ((1, 1), (1, 2), (2, 1)),
    ((2, 2), (0, 3), (3, 0)),
    ((3, 1), (3, 2), (1, 3), (2, 3), (3, 3)),
)
SEND_AFTER = ((3, 5), (2, 3), (1, 1), (2, 4))
FLAT = sum(NEW_BLOCKS, ())
BATCHES = tuple(FLAT[i:i + 2] for i in range(0, 16, 2))


def plus(*terms):
    total = terms[0].astype(F32)
    for term in terms[1:]:
        total = total + term.astype(F32)
    return total


class Rings:
    def __init__(self, refs, up, down, remote):
        (self.part, self.rp, self.rm, self.fp, self.fm, self.part2, self.rp2, self.rm2, self.fp2, self.fm2) = refs[:10]
        self.sems = refs[10:]
        self.up, self.down, self.remote = up, down, remote
        self.unit = self.part.shape[-2]

    def copy(self, which, h, g, k):
        part, sems = self.part, self.sems
        if which < 4:
            at, up, down = (h, g, k), self.up[h], self.down[h]
            rp, rm, fp, fm = self.rp, self.rm, self.fp, self.fm
        else:
            part, at, up, down = self.part2, (h, g), self.up[1 - h], self.down[1 - h]
            rp, rm, fp, fm = self.rp2, self.rm2, self.fp2, self.fm2
        src, dst, to = (
            (part.at[(*at, pl.ds(0, 2))], rp.at[at], up),
            (part.at[(*at, pl.ds(2, 2))], rm.at[at], down),
            (rp.at[(*at, 0)], fp.at[at], up),
            (rm.at[(*at, 1)], fm.at[at], down),
        )[which % 4]
        return self.remote(src, dst, sems[2 * which].at[at], sems[2 * which + 1].at[at], to)

    def place(self, g, ry, rx, tile):
        u = self.unit
        self.part[0, g, ry, A_SLOT[rx]] = tile[:u]
        self.part[0, g, ry, B_SLOT[rx]] = tile[u:2 * u]
        self.part[1, g, rx, A_SLOT[ry]] = tile[2 * u:3 * u]
        self.part[1, g, rx, B_SLOT[ry]] = tile[3 * u:]

    def send(self, h, g, k):
        self.copy(0, h, g, k).start()
        self.copy(1, h, g, k).start()

    def forward(self, g, k):
        for h in range(2):
            self.copy(0, h, g, k).wait_recv()
            self.rp[h, g, k, 0] = plus(self.rp[h, g, k, 0], self.part[h, g, k, 4]).astype(BF)
            self.copy(2, h, g, k).start()
            self.copy(1, h, g, k).wait_recv()
            self.rm[h, g, k, 1] = plus(self.rm[h, g, k, 1], self.part[h, g, k, 5]).astype(BF)
            self.copy(3, h, g, k).start()

    def first_sum(self, g, k):
        for h in range(2):
            self.copy(2, h, g, k).wait_recv()
            self.copy(3, h, g, k).wait_recv()
            self.part2[h, g, A_SLOT[k]] = plus(
                self.part[h, g, k, 6], self.fp[h, g, k], self.rm[h, g, k, 0]).astype(BF)
            self.part2[h, g, B_SLOT[k]] = plus(
                self.part[h, g, k, 7], self.fm[h, g, k], self.rp[h, g, k, 1]).astype(BF)
            if k == 2:
                self.copy(4, h, g, 0).start()
                self.copy(5, h, g, 0).start()

    def forward2(self, g):
        for h in range(2):
            self.copy(4, h, g, 0).wait_recv()
            self.rp2[h, g, 0] = plus(self.rp2[h, g, 0], self.part2[h, g, 4]).astype(BF)
            self.copy(6, h, g, 0).start()
            self.copy(5, h, g, 0).wait_recv()
            self.rm2[h, g, 1] = plus(self.rm2[h, g, 1], self.part2[h, g, 5]).astype(BF)
            self.copy(7, h, g, 0).start()

    def second_sum(self, h, g):
        self.copy(6, h, g, 0).wait_recv()
        self.copy(7, h, g, 0).wait_recv()
        return [
            plus(self.part2[h, g, 6], self.fp2[h, g], self.rm2[h, g, 0]),
            plus(self.part2[h, g, 7], self.fm2[h, g], self.rp2[h, g, 1]),
        ]

    def drain(self, g):
        for h in range(2):
            for k in range(RING):
                for which in range(4):
                    self.copy(which, h, g, k).wait_send()
            for which in range(4, 8):
                self.copy(which, h, g, 0).wait_send()


class ShortRings(Rings):
    def __init__(self, refs, up, down, owners, remote):
        self.part, self.rp, self.rm, self.fp, self.fm, self.part2, self.got = refs[:7]
        self.sems, self.q_s, self.q_r = refs[7:15], refs[15], refs[16]
        self.up, self.down, self.owners, self.remote = up, down, owners, remote
        self.unit = self.part.shape[-2]

    def straight(self, h, k):
        return self.remote(
            self.part2.at[h, k], self.got.at[h, k], self.q_s.at[h, k], self.q_r.at[h, k], self.owners[1 - h][k])

    def first_sum(self, g, k):
        for h in range(2):
            self.copy(2, h, g, k).wait_recv()
            self.copy(3, h, g, k).wait_recv()
            self.part2[h, k, 0] = plus(self.part[h, g, k, 6], self.fp[h, g, k], self.rm[h, g, k, 0]).astype(BF)
            self.part2[h, k, 1] = plus(self.part[h, g, k, 7], self.fm[h, g, k], self.rp[h, g, k, 1]).astype(BF)
            if k < 3:
                self.straight(h, k).start()

    def second_sum(self, h, g):
        for k in range(3):
            self.straight(h, k).wait_recv()
        return [plus(self.part2[h, 3, i], *[self.got[h, k, i] for k in range(3)]) for i in range(2)]

    def drain(self, g):
        for h in range(2):
            for k in range(RING):
                for which in range(4):
                    self.copy(which, h, g, k).wait_send()
            for k in range(3):
                self.straight(h, k).wait_send()


def kernel(act, cot, weight, first_in, second_in, anchor_in, mom_in, exps_in,
           w_out, f_out, s_out, anc_out, mom_out,
           a_v, c_v, w_v, f_v, s_v, anc_v, mom_v, wo_v, fo_v, so_v, ao_v, mo_v,
           exps, wsum, rz, zt, zr, packs, pairs, totals,
           a_sem, c_sem, in_sem, out_sem, z_s, z_r, zx_s, zx_r, k_s, k_r, *ring_refs):
    groups = c_v.shape[1] // GW
    last = groups - 1
    own = w_v.shape[0]
    block = 2 * own
    rep = lax.axis_index("rep")
    f = lax.axis_index("fsdp")
    zhi, x, y = f % 2, (f // 2) % RING, f // (2 * RING)

    def dev(x=x, y=y, zhi=zhi, rep=rep):
        return (rep, (y * RING + x) * 2 + zhi)

    xp, xm = dev(x=(x + 1) % RING), dev(x=(x + RING - 1) % RING)
    yp, ym = dev(y=(y + 1) % RING), dev(y=(y + RING - 1) % RING)
    x2, y2 = dev(x=(x + 2) % RING), dev(y=(y + 2) % RING)
    zdev = dev(zhi=1 - zhi)
    zlo, core = rep // 2, rep % 2
    mate = dev(rep=2 * zlo + 1 - core)
    across = dev(rep=2 * (1 - zlo) + core)

    def cols(g):
        return pl.ds(pl.multiple_of(g * GW, GW), GW)

    def a_copy(blk):
        at = pl.ds(pl.multiple_of(blk * block, block), block)
        return pltpu.make_async_copy(act.at[0, :, at], a_v.at[:, at], a_sem.at[blk])

    def c_copy(g):
        return pltpu.make_async_copy(cot.at[0, :, cols(g)], c_v.at[:, cols(g)], c_sem.at[g])

    ins = [
        pltpu.make_async_copy(src, dst, in_sem.at[i])
        for i, (src, dst) in enumerate((
            (weight.at[0], w_v), (first_in.at[0], f_v), (second_in.at[0], s_v), (anchor_in, anc_v), (mom_in, mom_v),
            (exps_in, exps)))
    ]

    def inner_outs(g):
        return [
            pltpu.make_async_copy(src.at[:, cols(g)], dst.at[0, :, cols(g)], out_sem.at[i, g])
            for i, (src, dst) in enumerate(((wo_v, w_out), (fo_v, f_out), (so_v, s_out)))
        ]

    def outer_outs(g):
        return [
            pltpu.make_async_copy(src.at[:, cols(g)], dst.at[:, cols(g)], out_sem.at[3 + i, g])
            for i, (src, dst) in enumerate(((ao_v, anc_out), (mo_v, mom_out)))
        ]

    def remote(src, dst, s, r, to):
        return pltpu.make_async_remote_copy(
            src_ref=src, dst_ref=dst, send_sem=s, recv_sem=r, device_id=to, device_id_type=MESH)

    def c_z(g):
        return remote(wsum.at[1 - zhi, g], rz.at[g], z_s.at[g], z_r.at[g], zdev)

    def c_zx(ry, rx):
        return remote(zt.at[ry, rx, 1 - zhi], zr.at[ry, rx], zx_s.at[ry, rx], zx_r.at[ry, rx], zdev)

    def c_pack(g):
        here = packs.at[g, core, 1 - core]
        return remote(here, here, k_s.at[g, 0], k_r.at[g, 0], mate)

    def c_pair(g):
        here = pairs.at[g, zlo]
        return remote(here, here, k_s.at[g, 1], k_r.at[g, 1], across)

    def c_share(g):
        here = totals.at[g, core]
        return remote(here, here, k_s.at[g, 2], k_r.at[g, 2], mate)

    wide = Rings(ring_refs[:26], (xp, yp), (xm, ym), remote)
    thin = ShortRings(ring_refs[26:], (xp, yp), (xm, ym), ((x2, xp, xm), (y2, yp, ym)), remote)

    def product(g, ry, rx):
        blk = ((y + OFFS[ry]) % RING) * RING + (x + OFFS[rx]) % RING
        at = pl.ds(pl.multiple_of(blk * block, block), block)
        return lax.dot_general(
            a_v[:, at], c_v[:, cols(g)], (((0,), (0,)), ((), ())), preferred_element_type=F32).astype(BF)

    def products(g, k):
        @pl.when(g == 0)
        def _():
            for ry, rx in NEW_BLOCKS[k]:
                a_copy(((y + OFFS[ry]) % RING) * RING + (x + OFFS[rx]) % RING).wait()

        if k == 0:
            c_copy(g).wait()
        for n, (ry, rx) in enumerate(NEW_BLOCKS[k]):
            wide.place(g, ry, rx, product(g, ry, rx))
            for h in range(2):
                if n + 1 == SEND_AFTER[k][h]:
                    if k == 0 and h == 0:
                        @pl.when(g == 0)
                        def _():
                            pl.semaphore_wait(barrier, len(everyone))
                    wide.send(h, g, k)
        if k == 0:
            @pl.when(g == 0)
            def _():
                load_rest()

    def exchange(n):
        if n == 0:
            c_copy(last).wait()
        for ry, rx in BATCHES[n]:
            tile = product(last, ry, rx)
            zt[ry, rx, 0] = tile[:own]
            zt[ry, rx, 1] = tile[own:]
            c_zx(ry, rx).start()

    def products_last(g, k):
        for n, (ry, rx) in enumerate(NEW_BLOCKS[k]):
            c_zx(ry, rx).wait_recv()
            thin.place(0, ry, rx, plus(zt[ry, rx, zhi], zr[ry, rx]).astype(BF))
            for h in range(2):
                if n + 1 == SEND_AFTER[k][h]:
                    thin.send(h, 0, k)

    def second_sum(g):
        for h in range(2):
            wsum[h, g] = jnp.concatenate(wide.second_sum(h, g), axis=0).astype(BF)
        c_z(g).start()

    def powers(g):
        row = lax.broadcasted_iota(jnp.int32, (exps.shape[0], GW), 0)
        col = lax.broadcasted_iota(jnp.int32, (exps.shape[0], GW), 1)
        pick = jnp.where(row == g * (GW // 128) + col // 128, 1.0, 0.0).astype(BF)
        return lax.dot_general(
            exps[...].astype(F32).astype(BF), pick, (((0,), (0,)), ((), ())), preferred_element_type=F32)

    def adamw(g, grad):
        at = cols(g)
        first = (0.9 * f_v[:, at].astype(F32) + 0.1 * grad).astype(BF)
        second = (0.95 * s_v[:, at].astype(F32) + 0.05 * grad * grad).astype(BF)
        old = w_v[:, at].astype(F32)
        update = first.astype(F32) / (jnp.sqrt(second.astype(F32)) + 1e-08)
        fresh = (old - 0.1 * (update + 0.01 * old)).astype(BF)
        fo_v[:, at] = first
        so_v[:, at] = second
        wo_v[:, at] = fresh
        gap = anc_v[:, at].astype(F32) - fresh.astype(F32)
        pack = jnp.clip(gap * jnp.exp2(-powers(g)), -4.0, 4.0).astype(BF)
        packs[g, core, 0] = pack[:own // 2]
        packs[g, core, 1] = pack[own // 2:]
        c_pack(g).start()
        for copy in inner_outs(g):
            copy.start()

    def inner(g):
        c_z(g).wait_recv()
        @pl.when(g == 0)
        def _():
            for copy in ins:
                copy.wait()
        adamw(g, plus(wsum[zhi, g], rz[g]))

    def thin_forward(g, k):
        thin.forward(0, k)

    def thin_first_sum(g, k):
        thin.first_sum(0, k)

    def inner_last(g):
        adamw(last, jnp.concatenate(thin.second_sum(0, 0) + thin.second_sum(1, 0), axis=0))

    def pair(g):
        c_pack(g).wait_recv()
        pairs[g, zlo] = plus(packs[g, 0, core], packs[g, 1, core]).astype(BF)
        c_pair(g).start()

    def share(g):
        c_pair(g).wait_recv()
        totals[g, core] = plus(pairs[g, 0], pairs[g, 1])
        c_share(g).start()

    def outer(g):
        c_share(g).wait_recv()
        at = cols(g)
        total = jnp.concatenate([totals[g, 0], totals[g, 1]], axis=0)
        step = (jnp.exp2(powers(g)) * total) / REPS
        momentum = 0.9 * mom_v[:, at] + step
        mo_v[:, at] = momentum
        ao_v[:, at] = (anc_v[:, at].astype(F32) - 0.7 * (step + 0.9 * momentum)).astype(BF)
        for copy in outer_outs(g):
            copy.start()

    def tidy(g):
        wide.drain(g)
        c_z(g).wait_send()
        c_pack(g).wait_send()
        c_pair(g).wait_send()

    def tidy_last(g):
        thin.drain(0)
        for ry in range(RING):
            for rx in range(RING):
                c_zx(ry, rx).wait_send()
        c_pack(g).wait_send()
        c_pair(g).wait_send()

    before = last - 1
    ends = dict(
        forward=lambda: wide.forward2(before), sum=lambda: second_sum(before), inner=lambda: inner(before),
        pair=lambda: pair(before), share=lambda: share(before), outer=lambda: outer(before), tidy=lambda: tidy(before),
        inner_last=lambda: inner_last(last), pair_last=lambda: pair(last), share_last=lambda: share(last), outer_last=lambda: outer(last),
        tidy_last=lambda: tidy_last(last))

    everyone = [xp, xm, x2, yp, ym, y2, zdev, mate, across]
    barrier = pltpu.get_barrier_semaphore()
    for to in everyone:
        pl.semaphore_signal(barrier, inc=1, device_id=to, device_id_type=MESH)

    def load(k):
        for ry, rx in NEW_BLOCKS[k]:
            a_copy(((y + OFFS[ry]) % RING) * RING + (x + OFFS[rx]) % RING).start()

    def load_rest():
        for k in range(1, RING):
            load(k)
        for g in (last, *range(1, last)):
            c_copy(g).start()
        for copy in ins:
            copy.start()

    c_copy(0).start()
    load(0)

    def at_step(g, k, shift, stage, groups_of, *late):
        group, kk = g + (k + shift) // RING, (k + shift) % RING
        if not late or kk == RING - 1:
            @pl.when(groups_of(group))
            def _():
                stage(group) if late else stage(group, kk)

    def is_wide(group):
        return jnp.logical_and(group >= 0, group < last)

    def is_early(group):
        return jnp.logical_and(group >= 0, group < last - 1)

    def is_last(group):
        return group == last

    first_turn = -((max(LEADS) + RING - 1) // RING)
    last_turn = END[-1][0] // RING

    @pl.loop(0, groups - first_turn + last_turn)
    def _(turn):
        g = turn + first_turn
        for k in range(RING):
            at_step(g, k, LEADS[0], products, is_wide)
            at_step(g, k, LEADS[1], products_last, is_last)
            for n in range(len(BATCHES)):
                step = n + EXCHANGE
                if step % RING == k:
                    @pl.when(g == step // RING)
                    def _():
                        exchange(n)

            at_step(g, k, FLEADS[0], wide.forward, is_wide)
            at_step(g, k, FLEADS[1], thin_forward, is_last)
            at_step(g, k, 0, wide.first_sum, is_wide)
            at_step(g, k, 0, thin_first_sum, is_last)
            for lag, stage in zip(LAGS, (wide.forward2, second_sum, inner, pair, share, outer, tidy)):
                at_step(g, k, -lag, stage, is_early, "late")
            for step, stage in END:
                if step % RING == k:
                    @pl.when(g == last + step // RING)
                    def _():
                        ends[stage]()


    for g in range(groups):
        c_share(g).wait_send()
        for copy in inner_outs(g) + outer_outs(g):
            copy.wait()


def finish(*refs):
    given, made, held = refs[:5], refs[5:10], refs[10:15]
    sem = refs[15]
    inward = [pltpu.make_async_copy(given[i], held[i], sem.at[0, i]) for i in range(5)]
    outward = [pltpu.make_async_copy(held[i], made[i], sem.at[1, i]) for i in range(5)]
    for copy in inward:
        copy.start()
    for arrived, copy in zip(inward, outward):
        arrived.wait()
        copy.start()
    for copy in outward:
        copy.wait()


def local(activations, cotangent, weight, first_moment, second_moment, anchor, momentum, exponents):
    own, width = anchor.shape
    tokens, rows = activations.shape[1:]
    groups = width // GW
    dma = pltpu.SemaphoreType.DMA
    anywhere = pl.BlockSpec(memory_space=pl.ANY)

    def buf(*shape, kind=BF):
        return pltpu.VMEM(shape, kind)

    def rings(count, unit):
        return [
            buf(2, count, RING, 8, unit, GW),
            buf(2, count, RING, 2, unit, GW), buf(2, count, RING, 2, unit, GW),
            buf(2, count, RING, unit, GW), buf(2, count, RING, unit, GW),
            buf(2, count, 8, unit, GW),
            buf(2, count, 2, unit, GW), buf(2, count, 2, unit, GW),
            buf(2, count, unit, GW), buf(2, count, unit, GW),
        ] + [dma((2, count, RING))] * 8 + [dma((2, count))] * 8

    def short_rings(unit):
        return [
            buf(2, 1, RING, 8, unit, GW),
            buf(2, 1, RING, 2, unit, GW), buf(2, 1, RING, 2, unit, GW),
            buf(2, 1, RING, unit, GW), buf(2, 1, RING, unit, GW),
            buf(2, RING, 2, unit, GW), buf(2, RING - 1, 2, unit, GW),
        ] + [dma((2, 1, RING))] * 8 + [dma((2, RING - 1))] * 2

    outs = pl.pallas_call(
        kernel,
        out_shape=(
            jax.ShapeDtypeStruct(weight.shape, BF),
            jax.ShapeDtypeStruct(weight.shape, BF),
            jax.ShapeDtypeStruct(weight.shape, BF),
            jax.ShapeDtypeStruct(anchor.shape, BF),
            jax.ShapeDtypeStruct(momentum.shape, F32),
        ),
        in_specs=[anywhere] * 8,
        out_specs=[anywhere] * 5,
        scratch_shapes=[
            buf(tokens, rows), buf(tokens, width),
            buf(own, width), buf(own, width), buf(own, width), buf(own, width), buf(own, width, kind=F32),
            buf(own, width), buf(own, width), buf(own, width), buf(own, width), buf(own, width, kind=F32),
            buf(*exponents.shape[::-1], kind=jnp.int32),
            buf(2, groups - 1, own, GW), buf(groups - 1, own, GW),
            buf(RING, RING, 2, own, GW), buf(RING, RING, own, GW),
            buf(groups, 2, 2, own // 2, GW), buf(groups, 2, own // 2, GW), buf(groups, 2, own // 2, GW, kind=F32),
            dma((RING * RING,)), dma((groups,)), dma((6,)), dma((5, groups)),
            dma((groups - 1,)), dma((groups - 1,)), dma((RING, RING)), dma((RING, RING)),
            dma((groups, 3)), dma((groups, 3)),
        ] + rings(groups - 1, own // 2) + short_rings(own // 4),
        compiler_params=pltpu.CompilerParams(
            collective_id=0, has_side_effects=True, vmem_limit_bytes=58 * 1024 * 1024),
        cost_estimate=pl.CostEstimate(
            flops=2 * tokens * rows * width, bytes_accessed=12 * 2 ** 20, transcendentals=0),
        name="diloco_step",
    )(activations, cotangent, weight, first_moment, second_moment, anchor, momentum, exponents.T)
    return pl.pallas_call(
        finish,
        out_shape=[jax.ShapeDtypeStruct(o.shape, o.dtype) for o in outs],
        in_specs=[anywhere] * 5,
        out_specs=[anywhere] * 5,
        scratch_shapes=[buf(*o.shape, kind=o.dtype) for o in outs] + [dma((2, 5))],
        name="results",
    )(*outs)


def solution(mesh):
    split = P("rep", "fsdp", None)
    rows = P("fsdp", None)
    return jax.shard_map(
        local,
        mesh=mesh,
        in_specs=(split, split, split, split, split, rows, rows, rows),
        out_specs=(split, split, split, rows, rows),
        check_vma=False,
    )
```

```python
import jax
import jax.numpy as jnp
from jax import lax
from jax.experimental import pallas as pl
from jax.experimental.pallas import tpu as pltpu
from jax.sharding import PartitionSpec as P

MESH = pl.DeviceIdType.MESH
BF = jnp.bfloat16
F32 = jnp.float32

RING = 4
REPS = 4
GW = 256
LEADS = (4, 4)
FLEADS = (2, 2)
LAGS = (1, 3, 5, 6, 7, 7, 7)
END = ((0, "forward"), (1, "sum"), (3, "inner_last"), (3, "inner"), (4, "pair_last"), (4, "pair"), (4, "tidy_last"), (4, "tidy"), (4, "share_last"), (4, "share"), (4, "outer_last"), (4, "outer"))
EXCHANGE = -3
OFFS = (2, 1, 3, 0)
A_SLOT = (0, 4, 2, 6)
B_SLOT = (3, 1, 5, 7)
NEW_BLOCKS = (
    ((0, 0), (0, 1), (0, 2), (1, 0), (2, 0)),
    ((1, 1), (1, 2), (2, 1)),
    ((2, 2), (0, 3), (3, 0)),
    ((3, 1), (3, 2), (1, 3), (2, 3), (3, 3)),
)
SEND_AFTER = ((3, 5), (2, 3), (1, 1), (2, 4))
FLAT = sum(NEW_BLOCKS, ())
BATCHES = tuple(FLAT[i:i + 2] for i in range(0, 16, 2))


def plus(*terms):
    total = terms[0].astype(F32)
    for term in terms[1:]:
        total = total + term.astype(F32)
    return total


class Rings:
    def __init__(self, refs, up, down, remote):
        (self.part, self.rp, self.rm, self.fp, self.fm, self.part2, self.rp2, self.rm2, self.fp2, self.fm2) = refs[:10]
        self.sems = refs[10:]
        self.up, self.down, self.remote = up, down, remote
        self.unit = self.part.shape[-2]

    def copy(self, which, h, g, k):
        part, sems = self.part, self.sems
        if which < 4:
            at, up, down = (h, g, k), self.up[h], self.down[h]
            rp, rm, fp, fm = self.rp, self.rm, self.fp, self.fm
        else:
            part, at, up, down = self.part2, (h, g), self.up[1 - h], self.down[1 - h]
            rp, rm, fp, fm = self.rp2, self.rm2, self.fp2, self.fm2
        src, dst, to = (
            (part.at[(*at, pl.ds(0, 2))], rp.at[at], up),
            (part.at[(*at, pl.ds(2, 2))], rm.at[at], down),
            (rp.at[(*at, 0)], fp.at[at], up),
            (rm.at[(*at, 1)], fm.at[at], down),
        )[which % 4]
        return self.remote(src, dst, sems[2 * which].at[at], sems[2 * which + 1].at[at], to)

    def place(self, g, ry, rx, tile):
        u = self.unit
        self.part[0, g, ry, A_SLOT[rx]] = tile[:u]
        self.part[0, g, ry, B_SLOT[rx]] = tile[u:2 * u]
        self.part[1, g, rx, A_SLOT[ry]] = tile[2 * u:3 * u]
        self.part[1, g, rx, B_SLOT[ry]] = tile[3 * u:]

    def send(self, h, g, k):
        self.copy(0, h, g, k).start()
        self.copy(1, h, g, k).start()

    def forward(self, g, k):
        for h in range(2):
            self.copy(0, h, g, k).wait_recv()
            self.rp[h, g, k, 0] = plus(self.rp[h, g, k, 0], self.part[h, g, k, 4]).astype(BF)
            self.copy(2, h, g, k).start()
            self.copy(1, h, g, k).wait_recv()
            self.rm[h, g, k, 1] = plus(self.rm[h, g, k, 1], self.part[h, g, k, 5]).astype(BF)
            self.copy(3, h, g, k).start()

    def first_sum(self, g, k):
        for h in range(2):
            self.copy(2, h, g, k).wait_recv()
            self.copy(3, h, g, k).wait_recv()
            self.part2[h, g, A_SLOT[k]] = plus(
                self.part[h, g, k, 6], self.fp[h, g, k], self.rm[h, g, k, 0]).astype(BF)
            self.part2[h, g, B_SLOT[k]] = plus(
                self.part[h, g, k, 7], self.fm[h, g, k], self.rp[h, g, k, 1]).astype(BF)
            if k == 2:
                self.copy(4, h, g, 0).start()
                self.copy(5, h, g, 0).start()

    def forward2(self, g):
        for h in range(2):
            self.copy(4, h, g, 0).wait_recv()
            self.rp2[h, g, 0] = plus(self.rp2[h, g, 0], self.part2[h, g, 4]).astype(BF)
            self.copy(6, h, g, 0).start()
            self.copy(5, h, g, 0).wait_recv()
            self.rm2[h, g, 1] = plus(self.rm2[h, g, 1], self.part2[h, g, 5]).astype(BF)
            self.copy(7, h, g, 0).start()

    def second_sum(self, h, g):
        self.copy(6, h, g, 0).wait_recv()
        self.copy(7, h, g, 0).wait_recv()
        return [
            plus(self.part2[h, g, 6], self.fp2[h, g], self.rm2[h, g, 0]),
            plus(self.part2[h, g, 7], self.fm2[h, g], self.rp2[h, g, 1]),
        ]

    def drain(self, g):
        for h in range(2):
            for k in range(RING):
                for which in range(4):
                    self.copy(which, h, g, k).wait_send()
            for which in range(4, 8):
                self.copy(which, h, g, 0).wait_send()


class ShortRings(Rings):
    def __init__(self, refs, up, down, owners, remote):
        self.part, self.rp, self.rm, self.fp, self.fm, self.part2, self.got = refs[:7]
        self.sems, self.q_s, self.q_r = refs[7:15], refs[15], refs[16]
        self.up, self.down, self.owners, self.remote = up, down, owners, remote
        self.unit = self.part.shape[-2]

    def straight(self, h, k):
        return self.remote(
            self.part2.at[h, k], self.got.at[h, k], self.q_s.at[h, k], self.q_r.at[h, k], self.owners[1 - h][k])

    def first_sum(self, g, k):
        for h in range(2):
            self.copy(2, h, g, k).wait_recv()
            self.copy(3, h, g, k).wait_recv()
            self.part2[h, k, 0] = plus(self.part[h, g, k, 6], self.fp[h, g, k], self.rm[h, g, k, 0]).astype(BF)
            self.part2[h, k, 1] = plus(self.part[h, g, k, 7], self.fm[h, g, k], self.rp[h, g, k, 1]).astype(BF)
            if k < 3:
                self.straight(h, k).start()

    def second_sum(self, h, g):
        for k in range(3):
            self.straight(h, k).wait_recv()
        return [plus(self.part2[h, 3, i], *[self.got[h, k, i] for k in range(3)]) for i in range(2)]

    def drain(self, g):
        for h in range(2):
            for k in range(RING):
                for which in range(4):
                    self.copy(which, h, g, k).wait_send()
            for k in range(3):
                self.straight(h, k).wait_send()


def kernel(act, cot, weight, first_in, second_in, anchor_in, mom_in, exps_in,
           w_out, f_out, s_out, anc_out, mom_out,
           a_v, c_v, w_v, f_v, s_v, anc_v, mom_v, wo_v, fo_v, so_v, ao_v, mo_v,
           exps, wsum, rz, zt, zr, packs, pairs, totals,
           a_sem, c_sem, in_sem, out_sem, z_s, z_r, zx_s, zx_r, k_s, k_r, *ring_refs):
    groups = c_v.shape[1] // GW
    last = groups - 1
    own = w_v.shape[0]
    block = 2 * own
    rep = lax.axis_index("rep")
    f = lax.axis_index("fsdp")
    zhi, x, y = f % 2, (f // 2) % RING, f // (2 * RING)

    def dev(x=x, y=y, zhi=zhi, rep=rep):
        return (rep, (y * RING + x) * 2 + zhi)

    xp, xm = dev(x=(x + 1) % RING), dev(x=(x + RING - 1) % RING)
    yp, ym = dev(y=(y + 1) % RING), dev(y=(y + RING - 1) % RING)
    x2, y2 = dev(x=(x + 2) % RING), dev(y=(y + 2) % RING)
    zdev = dev(zhi=1 - zhi)
    zlo, core = rep // 2, rep % 2
    mate = dev(rep=2 * zlo + 1 - core)
    across = dev(rep=2 * (1 - zlo) + core)

    def cols(g):
        return pl.ds(pl.multiple_of(g * GW, GW), GW)

    def a_copy(blk):
        at = pl.ds(pl.multiple_of(blk * block, block), block)
        return pltpu.make_async_copy(act.at[0, :, at], a_v.at[:, at], a_sem.at[blk])

    def c_copy(g):
        return pltpu.make_async_copy(cot.at[0, :, cols(g)], c_v.at[:, cols(g)], c_sem.at[g])

    ins = [
        pltpu.make_async_copy(src, dst, in_sem.at[i])
        for i, (src, dst) in enumerate((
            (weight.at[0], w_v), (first_in.at[0], f_v), (second_in.at[0], s_v), (anchor_in, anc_v), (mom_in, mom_v),
            (exps_in, exps)))
    ]

    def inner_outs(g):
        return [
            pltpu.make_async_copy(src.at[:, cols(g)], dst.at[0, :, cols(g)], out_sem.at[i, g])
            for i, (src, dst) in enumerate(((wo_v, w_out), (fo_v, f_out), (so_v, s_out)))
        ]

    def outer_outs(g):
        return [
            pltpu.make_async_copy(src.at[:, cols(g)], dst.at[:, cols(g)], out_sem.at[3 + i, g])
            for i, (src, dst) in enumerate(((ao_v, anc_out), (mo_v, mom_out)))
        ]

    def remote(src, dst, s, r, to):
        return pltpu.make_async_remote_copy(
            src_ref=src, dst_ref=dst, send_sem=s, recv_sem=r, device_id=to, device_id_type=MESH)

    def c_z(g):
        return remote(wsum.at[1 - zhi, g], rz.at[g], z_s.at[g], z_r.at[g], zdev)

    def c_zx(ry, rx):
        return remote(zt.at[ry, rx, 1 - zhi], zr.at[ry, rx], zx_s.at[ry, rx], zx_r.at[ry, rx], zdev)

    def c_pack(g):
        here = packs.at[g, core, 1 - core]
        return remote(here, here, k_s.at[g, 0], k_r.at[g, 0], mate)

    def c_pair(g):
        here = pairs.at[g, zlo]
        return remote(here, here, k_s.at[g, 1], k_r.at[g, 1], across)

    def c_share(g):
        here = totals.at[g, core]
        return remote(here, here, k_s.at[g, 2], k_r.at[g, 2], mate)

    wide = Rings(ring_refs[:26], (xp, yp), (xm, ym), remote)
    thin = ShortRings(ring_refs[26:], (xp, yp), (xm, ym), ((x2, xp, xm), (y2, yp, ym)), remote)

    def product(g, ry, rx):
        blk = ((y + OFFS[ry]) % RING) * RING + (x + OFFS[rx]) % RING
        at = pl.ds(pl.multiple_of(blk * block, block), block)
        return lax.dot_general(
            a_v[:, at], c_v[:, cols(g)], (((0,), (0,)), ((), ())), preferred_element_type=F32).astype(BF)

    def products(g, k, first=False):
        if first:
            for ry, rx in NEW_BLOCKS[k]:
                a_copy(((y + OFFS[ry]) % RING) * RING + (x + OFFS[rx]) % RING).wait()
        elif k > 0:
            @pl.when(g == 0)
            def _():
                for ry, rx in NEW_BLOCKS[k]:
                    a_copy(((y + OFFS[ry]) % RING) * RING + (x + OFFS[rx]) % RING).wait()

        if k == 0:
            c_copy(g).wait()
        for n, (ry, rx) in enumerate(NEW_BLOCKS[k]):
            wide.place(g, ry, rx, product(g, ry, rx))
            for h in range(2):
                if n + 1 == SEND_AFTER[k][h]:
                    if first and h == 0:
                        pl.semaphore_wait(barrier, len(everyone))
                    wide.send(h, g, k)

    def exchange(n):
        if n == 0:
            c_copy(last).wait()
        for ry, rx in BATCHES[n]:
            tile = product(last, ry, rx)
            zt[ry, rx, 0] = tile[:own]
            zt[ry, rx, 1] = tile[own:]
            c_zx(ry, rx).start()

    def products_last(g, k):
        for n, (ry, rx) in enumerate(NEW_BLOCKS[k]):
            c_zx(ry, rx).wait_recv()
            thin.place(0, ry, rx, plus(zt[ry, rx, zhi], zr[ry, rx]).astype(BF))
            for h in range(2):
                if n + 1 == SEND_AFTER[k][h]:
                    thin.send(h, 0, k)

    def second_sum(g):
        for h in range(2):
            wsum[h, g] = jnp.concatenate(wide.second_sum(h, g), axis=0).astype(BF)
        c_z(g).start()

    def powers(g):
        row = lax.broadcasted_iota(jnp.int32, (exps.shape[0], GW), 0)
        col = lax.broadcasted_iota(jnp.int32, (exps.shape[0], GW), 1)
        pick = jnp.where(row == g * (GW // 128) + col // 128, 1.0, 0.0).astype(BF)
        return lax.dot_general(
            exps[...].astype(F32).astype(BF), pick, (((0,), (0,)), ((), ())), preferred_element_type=F32)

    def adamw(g, grad):
        at = cols(g)
        first = (0.9 * f_v[:, at].astype(F32) + 0.1 * grad).astype(BF)
        second = (0.95 * s_v[:, at].astype(F32) + 0.05 * grad * grad).astype(BF)
        old = w_v[:, at].astype(F32)
        update = first.astype(F32) / (jnp.sqrt(second.astype(F32)) + 1e-08)
        fresh = (old - 0.1 * (update + 0.01 * old)).astype(BF)
        fo_v[:, at] = first
        so_v[:, at] = second
        wo_v[:, at] = fresh
        gap = anc_v[:, at].astype(F32) - fresh.astype(F32)
        pack = jnp.clip(gap * jnp.exp2(-powers(g)), -4.0, 4.0).astype(BF)
        packs[g, core, 0] = pack[:own // 2]
        packs[g, core, 1] = pack[own // 2:]
        c_pack(g).start()
        for copy in inner_outs(g):
            copy.start()

    def inner(g):
        c_z(g).wait_recv()
        @pl.when(g == 0)
        def _():
            for copy in ins:
                copy.wait()
        adamw(g, plus(wsum[zhi, g], rz[g]))

    def thin_forward(g, k):
        thin.forward(0, k)

    def thin_first_sum(g, k):
        thin.first_sum(0, k)

    def inner_last(g):
        adamw(last, jnp.concatenate(thin.second_sum(0, 0) + thin.second_sum(1, 0), axis=0))

    def pair(g):
        c_pack(g).wait_recv()
        pairs[g, zlo] = plus(packs[g, 0, core], packs[g, 1, core]).astype(BF)
        c_pair(g).start()

    def share(g):
        c_pair(g).wait_recv()
        totals[g, core] = plus(pairs[g, 0], pairs[g, 1])
        c_share(g).start()

    def outer(g):
        c_share(g).wait_recv()
        at = cols(g)
        total = jnp.concatenate([totals[g, 0], totals[g, 1]], axis=0)
        step = (jnp.exp2(powers(g)) * total) / REPS
        momentum = 0.9 * mom_v[:, at] + step
        mo_v[:, at] = momentum
        ao_v[:, at] = (anc_v[:, at].astype(F32) - 0.7 * (step + 0.9 * momentum)).astype(BF)
        for copy in outer_outs(g):
            copy.start()

    def tidy(g):
        wide.drain(g)
        c_z(g).wait_send()
        c_pack(g).wait_send()
        c_pair(g).wait_send()

    def tidy_last(g):
        thin.drain(0)
        for ry in range(RING):
            for rx in range(RING):
                c_zx(ry, rx).wait_send()
        c_pack(g).wait_send()
        c_pair(g).wait_send()

    before = last - 1
    ends = dict(
        forward=lambda: wide.forward2(before), sum=lambda: second_sum(before), inner=lambda: inner(before),
        pair=lambda: pair(before), share=lambda: share(before), outer=lambda: outer(before), tidy=lambda: tidy(before),
        inner_last=lambda: inner_last(last), pair_last=lambda: pair(last), share_last=lambda: share(last), outer_last=lambda: outer(last),
        tidy_last=lambda: tidy_last(last))

    everyone = [xp, xm, x2, yp, ym, y2, zdev, mate, across]
    barrier = pltpu.get_barrier_semaphore()
    for to in everyone:
        pl.semaphore_signal(barrier, inc=1, device_id=to, device_id_type=MESH)

    def load(k):
        for ry, rx in NEW_BLOCKS[k]:
            a_copy(((y + OFFS[ry]) % RING) * RING + (x + OFFS[rx]) % RING).start()

    def load_rest():
        for k in range(1, RING):
            load(k)
        for g in (last, *range(1, last)):
            c_copy(g).start()
        for copy in ins:
            copy.start()

    c_copy(0).start()
    load(0)
    products(0, 0, first=True)
    load_rest()

    def at_step(g, k, shift, stage, groups_of, *late, after=0):
        group, kk = g + (k + shift) // RING, (k + shift) % RING
        if not late or kk == RING - 1:
            @pl.when(jnp.logical_and(groups_of(group), group * RING + kk >= after))
            def _():
                stage(group) if late else stage(group, kk)

    def is_wide(group):
        return jnp.logical_and(group >= 0, group < last)

    def is_early(group):
        return jnp.logical_and(group >= 0, group < last - 1)

    def is_last(group):
        return group == last

    first_turn = -((max(LEADS) + RING - 1) // RING)
    last_turn = END[-1][0] // RING

    @pl.loop(0, groups - first_turn + last_turn)
    def _(turn):
        g = turn + first_turn
        for k in range(RING):
            at_step(g, k, FLEADS[0], wide.forward, is_wide)
            at_step(g, k, FLEADS[1], thin_forward, is_last)
            at_step(g, k, LEADS[0], products, is_wide, after=1)
            at_step(g, k, LEADS[1], products_last, is_last)
            for n in range(len(BATCHES)):
                step = n + EXCHANGE
                if step % RING == k:
                    @pl.when(g == step // RING)
                    def _():
                        exchange(n)
            at_step(g, k, 0, wide.first_sum, is_wide)
            at_step(g, k, 0, thin_first_sum, is_last)
            for lag, stage in zip(LAGS, (wide.forward2, second_sum, inner, pair, share, outer, tidy)):
                at_step(g, k, -lag, stage, is_early, "late")
            for step, stage in END:
                if step % RING == k:
                    @pl.when(g == last + step // RING)
                    def _():
                        ends[stage]()


    for g in range(groups):
        c_share(g).wait_send()
        for copy in inner_outs(g) + outer_outs(g):
            copy.wait()


def finish(*refs):
    given, made, held = refs[:5], refs[5:10], refs[10:15]
    sem = refs[15]
    inward = [pltpu.make_async_copy(given[i], held[i], sem.at[0, i]) for i in range(5)]
    outward = [pltpu.make_async_copy(held[i], made[i], sem.at[1, i]) for i in range(5)]
    for copy in inward:
        copy.start()
    for arrived, copy in zip(inward, outward):
        arrived.wait()
        copy.start()
    for copy in outward:
        copy.wait()


def local(activations, cotangent, weight, first_moment, second_moment, anchor, momentum, exponents):
    own, width = anchor.shape
    tokens, rows = activations.shape[1:]
    groups = width // GW
    dma = pltpu.SemaphoreType.DMA
    anywhere = pl.BlockSpec(memory_space=pl.ANY)

    def buf(*shape, kind=BF):
        return pltpu.VMEM(shape, kind)

    def rings(count, unit):
        return [
            buf(2, count, RING, 8, unit, GW),
            buf(2, count, RING, 2, unit, GW), buf(2, count, RING, 2, unit, GW),
            buf(2, count, RING, unit, GW), buf(2, count, RING, unit, GW),
            buf(2, count, 8, unit, GW),
            buf(2, count, 2, unit, GW), buf(2, count, 2, unit, GW),
            buf(2, count, unit, GW), buf(2, count, unit, GW),
        ] + [dma((2, count, RING))] * 8 + [dma((2, count))] * 8

    def short_rings(unit):
        return [
            buf(2, 1, RING, 8, unit, GW),
            buf(2, 1, RING, 2, unit, GW), buf(2, 1, RING, 2, unit, GW),
            buf(2, 1, RING, unit, GW), buf(2, 1, RING, unit, GW),
            buf(2, RING, 2, unit, GW), buf(2, RING - 1, 2, unit, GW),
        ] + [dma((2, 1, RING))] * 8 + [dma((2, RING - 1))] * 2

    outs = pl.pallas_call(
        kernel,
        out_shape=(
            jax.ShapeDtypeStruct(weight.shape, BF),
            jax.ShapeDtypeStruct(weight.shape, BF),
            jax.ShapeDtypeStruct(weight.shape, BF),
            jax.ShapeDtypeStruct(anchor.shape, BF),
            jax.ShapeDtypeStruct(momentum.shape, F32),
        ),
        in_specs=[anywhere] * 8,
        out_specs=[anywhere] * 5,
        scratch_shapes=[
            buf(tokens, rows), buf(tokens, width),
            buf(own, width), buf(own, width), buf(own, width), buf(own, width), buf(own, width, kind=F32),
            buf(own, width), buf(own, width), buf(own, width), buf(own, width), buf(own, width, kind=F32),
            buf(*exponents.shape[::-1], kind=jnp.int32),
            buf(2, groups - 1, own, GW), buf(groups - 1, own, GW),
            buf(RING, RING, 2, own, GW), buf(RING, RING, own, GW),
            buf(groups, 2, 2, own // 2, GW), buf(groups, 2, own // 2, GW), buf(groups, 2, own // 2, GW, kind=F32),
            dma((RING * RING,)), dma((groups,)), dma((6,)), dma((5, groups)),
            dma((groups - 1,)), dma((groups - 1,)), dma((RING, RING)), dma((RING, RING)),
            dma((groups, 3)), dma((groups, 3)),
        ] + rings(groups - 1, own // 2) + short_rings(own // 4),
        compiler_params=pltpu.CompilerParams(
            collective_id=0, has_side_effects=True, vmem_limit_bytes=58 * 1024 * 1024),
        cost_estimate=pl.CostEstimate(
            flops=2 * tokens * rows * width, bytes_accessed=12 * 2 ** 20, transcendentals=0),
        name="diloco_step",
    )(activations, cotangent, weight, first_moment, second_moment, anchor, momentum, exponents.T)
    return pl.pallas_call(
        finish,
        out_shape=[jax.ShapeDtypeStruct(o.shape, o.dtype) for o in outs],
        in_specs=[anywhere] * 5,
        out_specs=[anywhere] * 5,
        scratch_shapes=[buf(*o.shape, kind=o.dtype) for o in outs] + [dma((2, 5))],
        name="results",
    )(*outs)


def solution(mesh):
    split = P("rep", "fsdp", None)
    rows = P("fsdp", None)
    return jax.shard_map(
        local,
        mesh=mesh,
        in_specs=(split, split, split, split, split, rows, rows, rows),
        out_specs=(split, split, split, rows, rows),
        check_vma=False,
    )
```
